32 devices in a mesh: src: 8 (over z, y), dst: 4 (over x, core).
Axes of the slice: x: 2, y: 2, z: 4, core: 2. Of those that a mesh axis runs over, the one named last changes fastest.
Arguments:
- features: float32 [4096, 256], P(('src', 'dst')), may hold values from -6 to 6
- source_weight: float32 [256, 256], replicated, may hold values from -0.375 to 0.375
- target_weight: float32 [256, 256], replicated, may hold values from -0.375 to 0.375
- attention_vector: float32 [4, 64], replicated, may hold values from -1.5 to 1.5
- attention_bias: float32 [256], replicated, may hold values from -3 to 3
- residual_weight: float32 [256, 256], replicated, may hold values from -0.375 to 0.375
- norm_gain: float32 [256], replicated, may hold values from 0.5 to 1.5
- norm_shift: float32 [256], replicated, may hold values from -3 to 3
- neighbours: int32 [8, 4, 8, 2], P('src', 'dst'), may hold values from 0 to 3, as said below
- slot_valid: int32 [8, 4, 8, 2], P('src', 'dst'), may hold values from 0 to 1, as said below
- edge_mask: int32 [8, 4, 8, 2, 128, 128], P('src', 'dst'), may hold values 0 or 1
- node_count: int32 [8, 4], replicated, may hold values from 64 to 128, as said below
- out_cotangent: float32 [4096, 256], P(('src', 'dst')), may hold values from -6 to 6
Outputs:
- output: float32 [4096, 256], P(('src', 'dst'))
- grad_features: float32 [4096, 256], P(('src', 'dst'))
- grad_source_weight: float32 [256, 256], replicated
- grad_target_weight: float32 [256, 256], replicated
- grad_attention_vector: float32 [4, 64], replicated
- grad_attention_bias: float32 [256], replicated
- grad_residual_weight: float32 [256, 256], replicated
- grad_norm_gain: float32 [256], replicated
- grad_norm_shift: float32 [256], replicated
The draws below stay inside these ranges and needn't reach their ends.
Inputs may be any that keep to these rules, and one draw needn't show every extreme that they name: `neighbours`: within one target block of one source index the 2 entries are distinct source block numbers. `slot_valid`: in every target block the valid slots come first and there is at least one; some target block has all 2 valid. The first node_count rows of a device's 128 rows are nodes, the rest padding; some device is full.
All inputs are finite; a program needn't handle non-finite values. No bound on the sum of `edge_mask` on one device may be relied on, other than what follows from the above.
Results may differ from the reference program's by a relative error of at most 0.0003.
Values sent between devices are 32-bit elements; how exact they have to be, the bound alone decides.
A program may use at most 64 MiB of HBM per device.

```python
import jax
import jax.numpy as jnp
from jax import lax

HEADS = 4
HEAD_DIM = 64
HID = 256
TILE = 128
SLOTS = 2
ROWS_DEV = 128
SRC_BLOCKS = 4
TGT_BLOCKS = 8
NODES = 4096
N_SRC = 8
N_DST = 4


def draw_neighbours(key, part):
    key = jax.random.fold_in(key, 11)
    ranks = jax.random.randint(key, (N_SRC, N_DST, TGT_BLOCKS, SRC_BLOCKS), 0, 4096, dtype=jnp.int32)
    ranks = ranks * SRC_BLOCKS + jnp.arange(SRC_BLOCKS, dtype=jnp.int32)
    order = jnp.argsort(ranks, axis=-1)
    return order[..., :SLOTS].astype(jnp.int32)


def draw_slot_valid(key, part):
    key = jax.random.fold_in(key, 23)
    first, second = jax.random.split(key)
    everyone = N_SRC * N_DST * TGT_BLOCKS
    counts = jax.random.randint(first, (N_SRC, N_DST, TGT_BLOCKS), 1, SLOTS + 1, dtype=jnp.int32)
    chosen = jax.random.randint(second, (), 0, everyone, dtype=jnp.int32)
    places = jnp.arange(everyone, dtype=jnp.int32).reshape(N_SRC, N_DST, TGT_BLOCKS)
    counts = jnp.where(places == chosen, SLOTS, counts)
    return (jnp.arange(SLOTS, dtype=jnp.int32)[None, None, None, :] < counts[..., None]).astype(jnp.int32)


def draw_node_count(key, part):
    key = jax.random.fold_in(key, 37)
    first, second = jax.random.split(key)
    counts = jax.random.randint(first, (N_SRC, N_DST), ROWS_DEV // 2, ROWS_DEV + 1, dtype=jnp.int32)
    chosen = jax.random.randint(second, (), 0, N_SRC * N_DST, dtype=jnp.int32)
    places = jnp.arange(N_SRC * N_DST, dtype=jnp.int32).reshape(N_SRC, N_DST)
    return jnp.where(places == chosen, ROWS_DEV, counts).astype(jnp.int32)


def plant(array, stream_key, smallest, largest):
    longest = array.shape.index(max(array.shape))
    spots = []
    for shift in (0, 1):
        where = [jax.random.randint(jax.random.fold_in(stream_key, axis), (), 0, length) for axis, length in enumerate(array.shape)]
        where[longest] = (where[longest] + shift) % array.shape[longest]
        spots.append(tuple(where))
    return array.at[spots[0]].set(smallest).at[spots[1]].set(largest)


def steps_of(stream_key, dims, shards, low, high):
    gain = 1.0
    for dim, blocks in shards:
        heights = jax.random.uniform(jax.random.fold_in(jax.random.fold_in(stream_key, 6), dim), (blocks,), jnp.float32, low / len(shards), high / len(shards))
        gain = gain * jnp.repeat(jnp.exp(heights), dims[dim] // blocks).reshape((-1,) + (1,) * (len(dims) - 1 - dim))
    return gain


def centred(key, dims, scale, most, shards=(), kind=jnp.bfloat16):
    entries = scale * jax.random.normal(key, dims, jnp.float32)
    if shards:
        entries = entries * steps_of(key, dims, shards, -0.22, 0.18)
    return jnp.clip(entries, -most, most).astype(kind)


def setup_inputs(seed: int = 0) -> dict:
    keys = jax.random.split(jax.random.key(seed), 14)
    features = centred(keys[0], (NODES, HID), 1.0, 6.0, ((0, 32),), jnp.float32)
    source_weight = centred(keys[1], (HID, HID), HID ** -0.5, 0.375, (), jnp.float32)
    target_weight = centred(keys[2], (HID, HID), HID ** -0.5, 0.375, (), jnp.float32)
    attention_vector = centred(keys[3], (HEADS, HEAD_DIM), 0.25, 1.5, (), jnp.float32)
    attention_bias = centred(keys[4], (HID,), 0.5, 3.0, (), jnp.float32)
    residual_weight = centred(keys[5], (HID, HID), HID ** -0.5, 0.375, (), jnp.float32)
    norm_gain = jnp.clip(1.0 + 0.1 * jax.random.normal(keys[6], (HID,), jnp.float32), 0.5, 1.5)
    norm_shift = centred(keys[7], (HID,), 0.5, 3.0, (), jnp.float32)
    neighbours = draw_neighbours(jax.random.fold_in(keys[13], 71), 0)
    slot_valid = draw_slot_valid(jax.random.fold_in(keys[13], 71), 0)
    edge_mask = plant((jax.random.randint(keys[10], (N_SRC, N_DST, TGT_BLOCKS, SLOTS, TILE, TILE), 0, 16) < 1).astype(jnp.int32), jax.random.fold_in(keys[10], 1), 0, 1)
    node_count = draw_node_count(jax.random.fold_in(keys[13], 71), 0)
    out_cotangent = centred(keys[12], (NODES, HID), 1.0, 6.0, ((0, 32),), jnp.float32)
    return dict(features=features, source_weight=source_weight, target_weight=target_weight, attention_vector=attention_vector, attention_bias=attention_bias, residual_weight=residual_weight, norm_gain=norm_gain, norm_shift=norm_shift, neighbours=neighbours, slot_valid=slot_valid, edge_mask=edge_mask, node_count=node_count, out_cotangent=out_cotangent)


HIGH = lax.Precision.HIGHEST
NEGATIVE = -1e+30
EPSILON = 1e-05

@jax.custom_vjp
def low(v):
    return lax.optimization_barrier(v.astype(jnp.bfloat16)).astype(jnp.float32)

@jax.custom_vjp
def low_back(v):
    return v

def low_keep(v):
    return (low(v), None)

def low_pass(kept, grad):
    return (grad,)

def back_keep(v):
    return (v, None)

def back_low(kept, grad):
    return (low(grad),)
low.defvjp(low_keep, low_pass)
low_back.defvjp(back_keep, back_low)

def scores(target_rows, source_rows, attention_vector):
    joined = jax.nn.silu(target_rows[:, None, :] + source_rows[None, :, :])
    joined = joined.reshape(joined.shape[0], joined.shape[1], HEADS, HEAD_DIM)
    return jnp.einsum('tmhc,hc->htm', joined, attention_vector, precision=HIGH)

def forward(features, source_weight, target_weight, attention_vector, attention_bias, residual_weight, norm_gain, norm_shift, neighbours, slot_valid, edge_mask, node_count):
    source = jnp.dot(features, source_weight, precision=HIGH)
    target = jnp.dot(features, target_weight, precision=HIGH)
    residual = jnp.dot(features, residual_weight, precision=HIGH)
    source_span = ROWS_DEV * N_DST
    target_span = ROWS_DEV * N_SRC
    by_source = source.reshape(N_SRC, source_span, HID)
    target_view = target.reshape(N_SRC, N_DST, ROWS_DEV, HID).transpose(1, 0, 2, 3).reshape(N_DST, target_span, HID)
    self_view = source.reshape(N_SRC, N_DST, ROWS_DEV, HID).transpose(1, 0, 2, 3).reshape(N_DST, target_span, HID)
    positions = jnp.arange(source_span, dtype=jnp.int32)
    source_ok = positions[None, :] % ROWS_DEV < node_count[:, positions // ROWS_DEV]
    flat_vector = attention_vector.reshape(-1)

    def one_block(index):
        column = index // TGT_BLOCKS
        block = index % TGT_BLOCKS
        target_rows = lax.dynamic_slice_in_dim(target_view[column], block * TILE, TILE, 0)
        self_rows = lax.dynamic_slice_in_dim(self_view[column], block * TILE, TILE, 0)
        picks = neighbours[:, column, block, :]
        offsets = (picks[:, :, None] * TILE + jnp.arange(TILE, dtype=jnp.int32)[None, None, :]).reshape(N_SRC, SLOTS * TILE)
        gathered = jax.vmap(lambda table, rows: table[rows])(by_source, offsets)
        allowed = jax.vmap(lambda flags, rows: flags[rows])(source_ok, offsets)
        tile_mask = edge_mask[:, column, block] * slot_valid[:, column, block][:, :, None, None]
        live = (tile_mask.transpose(0, 2, 1, 3).reshape(N_SRC, TILE, SLOTS * TILE) > 0) & allowed[:, None, :]
        logits = lax.map(jax.checkpoint(lambda pair: scores(target_rows, pair, attention_vector)), gathered)
        masked = jnp.where(live[:, None], logits, NEGATIVE)
        self_logit = lax.optimization_barrier(jnp.sum((jax.nn.silu(target_rows + self_rows) * flat_vector).reshape(TILE, HEADS, HEAD_DIM), axis=2)).T
        top = jnp.maximum(lax.optimization_barrier(jnp.max(masked, axis=(0, 3))), self_logit)
        weights = jnp.where(live[:, None], jnp.exp(masked - top[None, :, :, None]), 0.0)
        self_weight = jnp.exp(self_logit - top)
        total = lax.optimization_barrier(jnp.sum(weights, axis=(0, 3))) + self_weight
        values = gathered.reshape(N_SRC, SLOTS * TILE, HEADS, HEAD_DIM)
        summed = jnp.einsum('shtm,smhc->thc', weights, values, precision=HIGH)
        summed = summed + self_weight.T[:, :, None] * self_rows.reshape(TILE, HEADS, HEAD_DIM)
        return (summed / total.T[:, :, None]).reshape(TILE, HID)
    blocks = lax.map(jax.checkpoint(one_block), jnp.arange(N_DST * TGT_BLOCKS, dtype=jnp.int32))
    aggregated = blocks.reshape(N_DST, N_SRC, ROWS_DEV, HID).transpose(1, 0, 2, 3).reshape(NODES, HID)
    mixed = aggregated + attention_bias + residual
    center = mixed - lax.optimization_barrier(jnp.mean(mixed, axis=1, keepdims=True))
    scale = lax.rsqrt(lax.optimization_barrier(jnp.mean(center * center, axis=1, keepdims=True)) + EPSILON)
    normed = center * scale * norm_gain + norm_shift
    rows = jnp.arange(NODES, dtype=jnp.int32)
    keep = rows % ROWS_DEV < node_count.reshape(-1)[rows // ROWS_DEV]
    return jax.nn.elu(normed) * keep[:, None].astype(jnp.float32)

def reference(features, source_weight, target_weight, attention_vector, attention_bias, residual_weight, norm_gain, norm_shift, neighbours, slot_valid, edge_mask, node_count, out_cotangent):

    def apply(*params):
        return forward(*params, neighbours, slot_valid, edge_mask, node_count)
    output, pullback = jax.vjp(apply, features, source_weight, target_weight, attention_vector, attention_bias, residual_weight, norm_gain, norm_shift)
    grads = pullback(out_cotangent)
    return (output, grads[0], grads[1], grads[2], grads[3], grads[4], grads[5], grads[6], grads[7])
```

```python
import functools

import jax
import jax.numpy as jnp
from jax import lax
from jax.experimental import pallas as pl
from jax.experimental.pallas import tpu as pltpu
from jax.sharding import PartitionSpec as P

HIGH = lax.Precision.HIGHEST
NEGATIVE = -1e30
EPSILON = 1e-05
RANKS = 4
STAGES = 3
LARGEST = 1e26
F32 = jnp.float32
BF16 = jnp.bfloat16
VMEM = pltpu.VMEM
SMEM = pltpu.SMEM


def iota(shape, axis):
    return lax.broadcasted_iota(jnp.int32, shape, axis)


def split(values):
    high = values.astype(BF16)
    return high, (values - high.astype(F32)).astype(BF16)


def dot(left, right, precision=None):
    return jnp.dot(left, right, preferred_element_type=F32, precision=precision)


def dot_lanes(left, right, precision=None):
    return lax.dot_general(
        left, right, (((1,), (1,)), ((), ())), preferred_element_type=F32, precision=precision
    )


def split3(values):
    high, rest = split_off(values)
    middle, rest = split_off(rest)
    return high, middle, rest.astype(BF16)


def split_off(values):
    high = values.astype(BF16)
    return high, values - high.astype(F32)


def head_rows(values, heads):
    size = values.shape[0] // heads
    return jnp.concatenate(
        [jnp.sum(values[h * size : (h + 1) * size], axis=0, keepdims=True) for h in range(heads)], 0
    )


def spread(rows, hidden):
    heads, wide = rows.shape
    return jnp.concatenate(
        [jnp.broadcast_to(rows[h : h + 1], (hidden // heads, wide)) for h in range(heads)], 0
    )


def upright(row, tile):
    return jnp.broadcast_to(row, (tile, row.shape[1])).T


def row_table(values, info):
    return jnp.concatenate([*(part.astype(F32) for part in split3(values)), info], 0).astype(BF16)


def build_ranks(mask_ref, counts, rows, tile, slots):
    parts = []
    for slot in range(slots):
        shape = (tile, tile)
        near = iota(shape, 1).astype(F32) < counts[slot : slot + 1]
        live = (mask_ref[slot] != 0) & near & (iota(shape, 0) < rows)
        parts.append(live.astype(F32).T)
    live = jnp.concatenate(parts, 0)
    wide = slots * tile
    before = (iota((wide, wide), 1) <= iota((wide, wide), 0)).astype(F32).astype(BF16)
    ranks = live * dot(before, live.astype(BF16))
    degree = dot(jnp.ones((8, wide), BF16), live.astype(BF16))
    pieces = jnp.floor((degree + (RANKS - 1)) * (1.0 / RANKS))
    earlier = (iota((tile, tile), 0) < iota((tile, tile), 1)).astype(F32).astype(BF16)
    start = dot(pieces.astype(BF16), earlier)
    end = start + pieces
    coarse = jnp.floor(start * (1.0 / 64.0))
    row = iota((8, tile), 0)
    info = jnp.where(row == 0, degree, jnp.where(row == 1, coarse, start - 64.0 * coarse))
    chunks = (jnp.max(end).astype(jnp.int32) + (tile - 1)) // tile
    return ranks.astype(BF16), info, upright(start[0:1], tile), upright(end[0:1], tile), chunks


MESH = pl.DeviceIdType.MESH


def grid_of(sources):
    depth = 4 if sources % 4 == 0 else 1
    return depth, sources // depth


def greet(peers):
    barrier = pltpu.get_barrier_semaphore()
    for peer in peers:
        pl.semaphore_signal(barrier, inc=1, device_id=peer, device_id_type=MESH)
    pl.semaphore_wait(barrier, len(peers))


def remote(source, target, send, recv, peer):
    return pltpu.make_async_remote_copy(
        src_ref=source, dst_ref=target, send_sem=send, recv_sem=recv,
        device_id=peer, device_id_type=MESH,
    )


def line_peers(me, depth, width):
    line, lane = me // width, me % width
    return [{"src": lax.rem(line + k, depth) * width + lane} for k in range(1, depth)]


def lane_peers(me, width):
    line, lane = me // width, me % width
    return [{"src": line * width + lax.rem(lane + k, width)} for k in range(1, width)]


def src_peers(me, sources):
    return [{"src": lax.rem(me + k, sources)} for k in range(1, sources)]


def dst_peers(column, columns):
    return [{"dst": lax.rem(column + k, columns)} for k in range(1, columns)]


def beside(me, depth, width):
    line, lane = me // width, me % width
    up = {"src": jnp.minimum(line + 1, depth - 1) * width + lane}
    down = {"src": jnp.maximum(line - 1, 0) * width + lane}
    return line, up, down


def start_gather(own, pieces, me, depth, width, send, recv):
    line, up, down = beside(me, depth, width)
    mine = pieces.at[line]

    @pl.when(line < depth - 1)
    def _():
        remote(own, mine, send.at[0, 0], recv.at[line], up).start()

    @pl.when(line > 0)
    def _():
        remote(own, mine, send.at[0, 1], recv.at[line], down).start()


def relay_gather(pieces, me, depth, width, send, recv, distance, use):
    line, up, down = beside(me, depth, width)
    for below in (True, False):
        origin = line - distance if below else line + distance
        there = line >= distance if below else line + distance < depth
        place = 2 * distance - 1 if below else 2 * distance

        @pl.when(there)
        def _():
            piece = pieces.at[origin]
            remote(piece, piece, send.at[0, 0], recv.at[origin], up).wait_recv()

            @pl.when(line < depth - 1 if below else line > 0)
            def _():
                remote(piece, piece, send.at[place, 0], recv.at[origin], up if below else down).start()

            use(origin)


def finish_gather(own, pieces, me, depth, width, send, recv):
    line, up, down = beside(me, depth, width)
    mine = pieces.at[line]

    def sent(place, way):
        remote(mine if place else own, mine, send.at[place, way], recv.at[line], up).wait_send()

    @pl.when(line < depth - 1)
    def _():
        sent(0, 0)

    @pl.when(line > 0)
    def _():
        sent(0, 1)

    for distance in range(1, depth):
        for below in (True, False):
            there = line >= distance if below else line + distance < depth
            place = 2 * distance - 1 if below else 2 * distance

            @pl.when(there & (line < depth - 1 if below else line > 0))
            def _():
                sent(place, 0)


def gather_semaphores(depth):
    return [pltpu.SemaphoreType.DMA((2 * depth - 1, 2)), pltpu.SemaphoreType.DMA((depth,))]


def order_of(line, depth, step):
    return jnp.where(line < depth // 2, depth - 1 - step, step)


def send_ends(blocks, climbed, fallen, me, depth, width, sems):
    line, up, down = beside(me, depth, width)
    up_send, up_recv, down_send, down_recv = sems
    for step in range(depth - 1):

        @pl.when(line == 0)
        def _():
            far = depth - 1 - step
            remote(blocks.at[far], climbed.at[far], up_send.at[far], up_recv.at[far], up).start()

        @pl.when(line == depth - 1)
        def _():
            remote(blocks.at[step], fallen.at[step], down_send.at[step], down_recv.at[step], down).start()


def pass_along(blocks, work, climbed, fallen, me, depth, width, sems, step, merge):
    if step >= depth:
        return
    line, up, down = beside(me, depth, width)
    up_send, up_recv, down_send, down_recv = sems
    far = order_of(line, depth, step)
    inside = (line > 0) & (line < depth - 1)

    @pl.when(inside & (far > line))
    def _():
        copy = remote(work.at[far], climbed.at[far], up_send.at[far], up_recv.at[far], up)
        copy.wait_recv()
        work[far] = merge([climbed[far], blocks[far]])
        copy.start()

    @pl.when(inside & (far < line))
    def _():
        copy = remote(work.at[far], fallen.at[far], down_send.at[far], down_recv.at[far], down)
        copy.wait_recv()
        work[far] = merge([fallen[far], blocks[far]])
        copy.start()


def arrive(climbed, fallen, me, depth, width, sems):
    line, up, down = beside(me, depth, width)
    up_send, up_recv, down_send, down_recv = sems

    @pl.when(line > 0)
    def _():
        piece = climbed.at[line]
        remote(piece, piece, up_send.at[line], up_recv.at[line], up).wait_recv()

    @pl.when(line < depth - 1)
    def _():
        piece = fallen.at[line]
        remote(piece, piece, down_send.at[line], down_recv.at[line], down).wait_recv()


def finish_reduce(work, climbed, fallen, me, depth, width, sems):
    line, up, down = beside(me, depth, width)
    up_send, up_recv, down_send, down_recv = sems
    for far in range(depth):

        @pl.when(far > line)
        def _():
            remote(work.at[far], climbed.at[far], up_send.at[far], up_recv.at[far], up).wait_send()

        @pl.when(far < line)
        def _():
            remote(work.at[far], fallen.at[far], down_send.at[far], down_recv.at[far], down).wait_send()


def reduce_scratch(depth, rows, hidden):
    dma = pltpu.SemaphoreType.DMA
    return [
        VMEM((depth, rows, hidden), F32), VMEM((depth, rows, hidden), F32),
        VMEM((depth, rows, hidden), F32),
        dma((depth,)), dma((depth,)), dma((depth,)), dma((depth,)),
    ]


def start_small(own, slots, me, depth, width, send, recv):
    for k, peer in enumerate(line_peers(me, depth, width)):
        remote(own, slots.at[me // width], send.at[k], recv.at[me // width], peer).start()


def wait_small(own, slots, me, depth, width, send, recv):
    for k, peer in enumerate(line_peers(me, depth, width)):
        other = lax.rem(me // width + k + 1, depth)
        remote(own, slots.at[other], send.at[k], recv.at[other], peer).wait_recv()


def finish_small(own, slots, me, depth, width, send, recv):
    for k, peer in enumerate(line_peers(me, depth, width)):
        remote(own, slots.at[me // width], send.at[k], recv.at[me // width], peer).wait_send()


def small_semaphores(depth):
    return [pltpu.SemaphoreType.DMA((max(depth - 1, 1),)), pltpu.SemaphoreType.DMA((depth,))]


def gather_kernel(
    picks, valid, counts, vector_ref, features_ref, mask_ref, source_weight_ref, target_weight_ref,
    by_line_ref, by_side_ref, target_ref, source_ref, turned_ref, info_ref, bounds_ref, row_ref,
    selfs_ref, own_source_ref, own_target_ref, vector_out_ref, chunks_ref, picks_ref,
    masks, tiles, own_tiles, source_weight, target_weight, own_self, local, own_masks,
    send, recv, side_send, side_recv, pass_send, mask_send, mask_recv, tile_send, tile_recv,
    self_send, self_recv, *, sources, columns, heads,
):
    me, column = lax.axis_index("src"), lax.axis_index("dst")
    depth, width = grid_of(sources)
    line, lane = me // width, me % width
    _, slots, tile, _ = mask_ref.shape
    hidden = features_ref.shape[1]
    sideways, lanes = dst_peers(column, columns), lane_peers(me, width)
    here = lane * columns + column
    loads = [
        pltpu.make_async_copy(one, other, local.at[index])
        for index, (one, other) in enumerate(
            (
                (features_ref, by_line_ref.at[line]),
                (features_ref, by_side_ref.at[here]),
                (source_weight_ref, source_weight),
                (target_weight_ref, target_weight),
            )
        )
    ]
    mask_loads = [
        pltpu.make_async_copy(mask_ref.at[far * width + lane], masks.at[lane, far], own_masks.at[far])
        for far in range(depth)
    ]
    for load in [*loads, *mask_loads]:
        load.start()

    def tile_of(other):
        shape = (2 * depth * slots, tile)
        row = iota(shape, 0)
        total = jnp.zeros(shape, F32)
        for far in range(depth):
            block = far * width + other
            for slot in range(slots):
                pick = picks[slot, block]
                have = valid[slot, block] * counts[pick, me]
                place = far * slots + slot
                total = jnp.where(row == place, have.astype(F32), total)
                total = jnp.where(row == place + depth * slots, pick.astype(F32), total)
        return total

    tiles[lane] = tile_of(lane)
    for k in range(1, width):
        own_tiles[k - 1] = tile_of(lax.rem(lane + k, width))
    greet([*line_peers(me, depth, width), *lanes, *sideways])

    start_gather(features_ref, by_line_ref, me, depth, width, send, recv)
    own_slot = by_side_ref.at[here]
    for k, peer in enumerate([*sideways, *lanes]):
        remote(features_ref, own_slot, side_send.at[k], side_recv.at[here], peer).start()
    for k, peer in enumerate(lanes):
        other = lax.rem(lane + k + 1, width)
        remote(own_tiles.at[k], tiles.at[lane], tile_send.at[k], tile_recv.at[lane], peer).start()
        for far in range(depth):
            remote(
                mask_ref.at[far * width + other], masks.at[lane, far], mask_send.at[k, far],
                mask_recv.at[lane, far], peer,
            ).start()

    def keep(to_ref, index, values):
        high, low = split(values * 0.5)
        to_ref[index, :, :tile] = high
        to_ref[index, :, tile:] = low

    def project_target(index):
        keep(target_ref, index, dot_lanes(target_weight[...], by_line_ref[index], HIGH))

    def project_source(index):
        keep(source_ref, index, dot_lanes(source_weight[...], by_side_ref[index], HIGH))

    def rank(other, far):
        pair = other * depth + far
        tile_here = tiles[other]
        ranks, info, start, end, chunks = build_ranks(
            masks.at[other, far], tile_here[far * slots : (far + 1) * slots],
            counts[column, far * width + lane], tile, slots,
        )
        turned_ref[pair] = ranks
        info_ref[pair] = info
        bounds_ref[pair, 0] = start
        bounds_ref[pair, 1] = end
        chunks_ref[pair] = chunks
        for slot in range(slots):
            place = depth * slots + far * slots + slot
            pick = jnp.max(tile_here[place : place + 1])
            picks_ref[pair * slots + slot] = pick.astype(jnp.int32)

    for load in loads:
        load.wait()
    source_weight[...] = source_weight[...].T
    target_weight[...] = target_weight[...].T
    row = jnp.concatenate([vector_ref[head : head + 1, :] for head in range(heads)], 1)
    vector = upright(row, tile)
    vector_out_ref[...] = vector
    own = by_line_ref[line]
    own_source = dot_lanes(source_weight[...], own, HIGH)
    own_target = dot_lanes(target_weight[...], own, HIGH)
    own_source_ref[...] = own_source
    own_target_ref[...] = own_target
    half = 0.5 * (own_source + own_target)
    active = (half * jnp.tanh(half) + half) * vector
    own_self[...] = jnp.concatenate(
        [head_rows(active, heads), jnp.zeros((8 - heads, tile), F32)], 0
    )
    selfs_ref[line] = own_self[...]
    start_small(own_self, selfs_ref, me, depth, width, self_send, self_recv)
    keep(source_ref, here, own_source)
    keep(target_ref, line, own_target)

    def pass_sideways():
        for k in range(1, width):
            index = lax.rem(lane + k, width) * columns + column
            piece = by_side_ref.at[index]
            remote(piece, piece, side_send.at[0], side_recv.at[index], {"dst": column}).wait_recv()
            for j, peer in enumerate(sideways):
                remote(piece, piece, pass_send.at[k - 1, j], side_recv.at[index], peer).start()

    def take_side(index):
        piece = by_side_ref.at[index]
        remote(piece, piece, side_send.at[0], side_recv.at[index], {"dst": column}).wait_recv()
        project_source(index)

    def rank_other(k, far):
        other = lax.rem(lane + k, width)
        mask = masks.at[other, far]
        remote(mask, mask, mask_send.at[0, 0], mask_recv.at[other, far], {"dst": column}).wait_recv()
        rank(other, far)

    def relay(distance):
        if distance < depth:
            relay_gather(by_line_ref, me, depth, width, send, recv, distance, project_target)

    for load in mask_loads:
        load.wait()
    rank(lane, 0)
    relay(1)
    pass_sideways()
    for k in range(1, width):
        project_source(lax.rem(lane + k, width) * columns + column)
    for far in range(1, depth // 2):
        rank(lane, far)
    for k in range(1, columns):
        take_side(lane * columns + lax.rem(column + k, columns))
    for k in range(1, width):
        other = lax.rem(lane + k, width)
        tile_slot = tiles.at[other]
        remote(
            tile_slot, tile_slot, tile_send.at[0], tile_recv.at[other], {"dst": column}
        ).wait_recv()
        rank_other(k, 0)
    relay(2)
    for far in range(max(depth // 2, 1), depth):
        rank(lane, far)
    for k in range(1, width):
        for far in range(1, depth // 2):
            rank_other(k, far)
    for distance in range(3, depth):
        relay(distance)
    for k in range(1, width):
        other = lax.rem(lane + k, width)
        for j in range(1, columns):
            take_side(other * columns + lax.rem(column + j, columns))
    for k in range(1, width):
        for far in range(max(depth // 2, 1), depth):
            rank_other(k, far)
    wait_small(own_self, selfs_ref, me, depth, width, self_send, self_recv)
    for pair in range(sources):
        row_ref[pair] = row_table(selfs_ref[pair % depth], info_ref[pair])
    finish_gather(features_ref, by_line_ref, me, depth, width, send, recv)
    finish_small(own_self, selfs_ref, me, depth, width, self_send, self_recv)
    for k, peer in enumerate([*sideways, *lanes]):
        remote(features_ref, own_slot, side_send.at[k], side_recv.at[here], peer).wait_send()
    for k, peer in enumerate(lanes):
        for j in range(columns - 1):
            remote(own_slot, own_slot, pass_send.at[k, j], side_recv.at[here], peer).wait_send()
        remote(own_tiles.at[k], tiles.at[lane], tile_send.at[k], tile_recv.at[lane], peer).wait_send()
        for far in range(depth):
            remote(
                mask_ref.at[far], masks.at[lane, far], mask_send.at[k, far], mask_recv.at[lane, far], peer
            ).wait_send()


def middle_kernel(
    counts, summed_ref, features_ref, source_ref, target_ref, info_ref,
    residual_weight_ref, vector_ref, bias_ref, gain_ref, shift_ref, cotangent_ref,
    output_ref, row_ref, grads_ref, own_target_ref, own_source_ref, rows_ref,
    residual_grad_ref, features_grad_ref,
    pieces, small, own_small, small_send, small_recv,
    gather_send, gather_recv, work, climbed, fallen, *sems, sources, heads,
):
    me, column = lax.axis_index("src"), lax.axis_index("dst")
    depth, width = grid_of(sources)
    line = me // width
    hidden, tile = source_ref.shape
    greet(line_peers(me, depth, width))

    def merge(parts):
        tops = [part[hidden : hidden + heads] for part in parts]
        top = functools.reduce(jnp.maximum, tops)
        keep = [jnp.exp(one - top) for one in tops]
        summed = sum(part[:hidden] * spread(one, hidden) for part, one in zip(parts, keep))
        total = sum(part[hidden + heads :] * one for part, one in zip(parts, keep))
        return jnp.concatenate([summed, top, total], 0)

    send_ends(summed_ref, climbed, fallen, me, depth, width, sems)
    nothing = jnp.where(
        (iota((hidden + 8, tile), 0) >= hidden) & (iota((hidden + 8, tile), 0) < hidden + heads),
        NEGATIVE, 0.0,
    )

    @pl.when(line == 0)
    def _():
        climbed[line] = nothing

    @pl.when(line == depth - 1)
    def _():
        fallen[line] = nothing

    source = source_ref[...]
    features = features_ref[...]
    vector = vector_ref[...]
    half = 0.5 * (source + target_ref[...])
    risen = 1.0 + jnp.tanh(half)
    active = half * risen
    slope = (risen + active * (2.0 - risen)) * (0.5 * vector)
    self_logit = head_rows(active * vector, heads)
    residual = dot_lanes(residual_weight_ref[...].T, features, HIGH) + upright(bias_ref[...], tile)
    gain = upright(gain_ref[...], tile)
    shift = upright(shift_ref[...], tile)
    real = (iota((hidden, tile), 1) < counts[column, me]).astype(F32)
    cotangent = cotangent_ref[...].T * real
    for step in range(depth):
        pass_along(summed_ref, work, climbed, fallen, me, depth, width, sems, step, merge)
    arrive(climbed, fallen, me, depth, width, sems)
    remote_part = merge([summed_ref[line], climbed[line], fallen[line]])
    remote_top = remote_part[hidden : hidden + heads]
    remote_total = remote_part[hidden + heads :]
    top = jnp.maximum(remote_top, self_logit)
    keep_remote = jnp.exp(remote_top - top)
    self_weight = jnp.exp(self_logit - top)
    denominator = remote_total * keep_remote + self_weight
    log_total = top + jnp.log(denominator)
    inverse = 1.0 / denominator
    self_alpha = spread(self_weight * inverse, hidden)
    keep_remote = spread(keep_remote * inverse, hidden)
    mixed = remote_part[:hidden] * keep_remote + source * self_alpha + residual

    def mean(values):
        return jnp.sum(values, axis=0, keepdims=True) * (1.0 / hidden)

    center = mixed - mean(mixed)
    scale = lax.rsqrt(mean(center * center) + EPSILON)
    unit = center * scale
    normed = unit * gain + shift
    below = jnp.exp(jnp.minimum(normed, 0.0))
    grad_normed = cotangent * jnp.where(normed > 0, 1.0, below)
    grad_unit = grad_normed * gain
    grad_mixed = scale * (grad_unit - mean(grad_unit) - unit * mean(grad_unit * unit))
    pieces[line] = grad_mixed
    own = pieces.at[line]
    start_gather(own, pieces, me, depth, width, gather_send, gather_recv)
    delta = head_rows(grad_mixed * (mixed - residual), heads)
    own_small[...] = jnp.concatenate([log_total, delta], 0)
    small[line] = own_small[...]
    start_small(own_small, small, me, depth, width, small_send, small_recv)

    def expand(index):
        high, low = split(pieces[index])
        grads_ref[index, :, :tile] = high
        grads_ref[index, :, tile:] = low

    expand(line)
    products = head_rows(grad_mixed * source, heads)
    grad_logit = self_alpha * spread(products - delta, hidden)
    grad_inner = grad_logit * slope
    own_target_ref[...] = grad_inner
    own_source_ref[...] = self_alpha * grad_mixed + grad_inner
    if depth > 1:
        relay_gather(pieces, me, depth, width, gather_send, gather_recv, 1, expand)
    output_ref[...] = (jnp.where(normed > 0, normed, below - 1.0) * real).T
    for index, values in enumerate(
        (grad_logit * active, grad_mixed, grad_normed * unit, grad_normed)
    ):
        rows_ref[index : index + 1, :] = dot_lanes(jnp.ones((8, tile), F32), values, HIGH)[0:1]
    rows_ref[4:, :] = jnp.zeros((4, hidden), F32)
    if depth > 2:
        relay_gather(pieces, me, depth, width, gather_send, gather_recv, 2, expand)
    residual_grad_ref[...] = dot(grad_mixed, features, HIGH)
    features_grad_ref[...] = dot(residual_weight_ref[...], grad_mixed, HIGH)
    wait_small(own_small, small, me, depth, width, small_send, small_recv)
    for pair in range(sources):
        row_ref[pair] = row_table(small[pair % depth], info_ref[pair])
    for distance in range(3, depth):
        relay_gather(pieces, me, depth, width, gather_send, gather_recv, distance, expand)
    finish_gather(own, pieces, me, depth, width, gather_send, gather_recv)
    finish_reduce(work, climbed, fallen, me, depth, width, sems)
    finish_small(own_small, small, me, depth, width, small_send, small_recv)


def exchange_stages(me, column, sources, columns):
    across = columns // 2
    half, core = column // 2, column % 2
    return [
        (2, core, lambda at: {"dst": half * 2 + at}),
        (across, half, lambda at: {"dst": at * 2 + core}),
        (sources, me, lambda at: {"src": at}),
    ]


def last_kernel(
    grad_target_ref, grad_source_ref, vector_grad_ref, rows_ref, by_line_ref, by_side_ref,
    residual_grad_ref, features_grad_ref, source_weight_ref, target_weight_ref,
    grad_features_ref, weights_ref, sums_ref,
    partial, parts, sums_in, part_send, part_recv, sum_send, sum_recv, full_send, full_recv,
    core_in, core_sum, core_send, core_recv, lane_in, lane_sum, lane_send, lane_recv,
    side_in, side_send, side_recv, work, climbed, fallen, *sems, sources, columns,
):
    me, column = lax.axis_index("src"), lax.axis_index("dst")
    depth, width = grid_of(sources)
    line, lane = me // width, me % width
    hidden, tile = features_grad_ref.shape
    rows = weights_ref.shape[1]
    stages = exchange_stages(me, column, sources, columns)
    greet([*src_peers(me, sources), *dst_peers(column, columns)])

    across, half, core = columns // 2, column // 2, column % 2
    lanes = lane_peers(me, width)

    def core_copy(other, side):
        place = other * across + side
        return remote(
            grad_source_ref.at[other * columns + side * 2 + 1 - core], core_in.at[place],
            core_send.at[place], core_recv.at[place], {"dst": half * 2 + 1 - core},
        )

    def lane_copy(k, side):
        other = lax.rem(lane + k + 1, width)
        place = k * across + side
        return remote(
            core_sum.at[other * across + side], lane_in.at[place], lane_send.at[place],
            lane_recv.at[place], lanes[k],
        )

    def side_copy(k):
        side = lax.rem(half + k, across)
        return remote(
            lane_sum.at[side], side_in.at[k - 1], side_send.at[k - 1], side_recv.at[k - 1],
            {"dst": side * 2 + core},
        )

    def end_core():
        for other in range(width):
            for side in range(across):
                core_copy(other, side).wait()
                place = other * across + side
                core_sum[place] = (
                    grad_source_ref[other * columns + side * 2 + core] + core_in[place]
                )
        for k in range(width - 1):
            for side in range(across):
                lane_copy(k, side).start()

    def end_lanes():
        for side in range(across):
            total = core_sum[lane * across + side]
            for k in range(width - 1):
                lane_copy(k, side).wait()
                total = total + lane_in[k * across + side]
            lane_sum[side] = total
        for k in range(1, across):
            side_copy(k).start()

    def end_sides():
        total = lane_sum[half]
        for k in range(1, across):
            side_copy(k).wait()
            total = total + side_in[k - 1]
        return total

    send_ends(grad_target_ref, climbed, fallen, me, depth, width, sems)
    for other in range(width):
        for side in range(across):
            core_copy(other, side).start()

    def over_rows(grad_ref, features_ref, count):
        total = jnp.zeros((hidden, hidden), F32)
        for index in range(count):
            high, low = split(grad_ref[index])
            large, small = split(features_ref[index])
            total = total + dot(
                jnp.concatenate([high, low, high], 1), jnp.concatenate([large, large, small], 0)
            )
        return total

    def fill(number, values):
        partial[number, :hidden, :] = values
        if rows > hidden:
            partial[number, hidden:, :] = jnp.zeros((rows - hidden, hidden), F32)

    offsets = [[jnp.int32(0)] for _ in range(3)]
    lengths = [rows]
    for size, _, _ in stages:
        lengths.append(lengths[-1] // size)

    def part_copies(number, index, waiting):
        size, place, peer_at = stages[index]
        part = lengths[index + 1]
        for k in range(1, size):
            at = lax.rem(place + k, size)
            start = pl.multiple_of(offsets[number][index] + at * part, 8)
            yield remote(
                partial.at[number, pl.ds(start, part), :], parts[index].at[number, k - 1],
                part_send[index].at[number, k - 1], part_recv[index].at[number, k - 1], peer_at(at),
            )
            if number == 0:
                yield remote(
                    sums_ref, sums_in[index].at[k - 1],
                    sum_send[index].at[k - 1], sum_recv[index].at[k - 1], peer_at(at),
                )

    def start_stage(number, index):
        for copy in part_copies(number, index, False):
            copy.start()

    def end_stage(number, index):
        size, place, _ = stages[index]
        part = lengths[index + 1]
        for copy in part_copies(number, index, True):
            copy.wait()
        start = pl.multiple_of(offsets[number][index] + place * part, 8)
        offsets[number].append(start)
        own = pl.ds(start, part)
        total = partial[number, own, :]
        for k in range(1, size):
            total = total + parts[index][number, k - 1]
        if index + 1 < len(stages):
            partial[number, own, :] = total
        else:
            weights_ref[number, own, :] = total
        if number == 0:
            sums = sums_ref[...]
            for k in range(1, size):
                sums = sums + sums_in[index][k - 1]
            sums_ref[...] = sums
        if index + 1 < len(stages):
            start_stage(number, index + 1)
        else:
            start_return(number, index)

    def return_copies(number, index, waiting):
        size, place, peer_at = stages[index]
        part = lengths[index + 1]
        for k in range(1, size):
            at = lax.rem(place + (size - k if waiting else 0), size)
            start = pl.multiple_of(offsets[number][index] + at * part, 8)
            segment = weights_ref.at[number, pl.ds(start, part), :]
            yield remote(
                segment, segment, full_send[index].at[number, k - 1],
                full_recv[index].at[number, k - 1], peer_at(lax.rem(place + k, size)),
            )

    def start_return(number, index):
        for copy in return_copies(number, index, False):
            copy.start()

    def end_return(number, index):
        for copy in return_copies(number, index, True):
            copy.wait()
        if index > 0:
            start_return(number, index - 1)

    def reduce_step(step):
        pass_along(
            grad_target_ref, work, climbed, fallen, me, depth, width, sems, step,
            lambda parts: parts[0] + parts[1],
        )

    nothing = jnp.zeros((hidden, tile), F32)

    @pl.when(line == 0)
    def _():
        climbed[line] = nothing

    @pl.when(line == depth - 1)
    def _():
        fallen[line] = nothing

    sums = rows_ref[...]
    first_row = (iota(sums.shape, 0) == 0).astype(F32)
    sums_ref[...] = sums + first_row * vector_grad_ref[...]
    fill(0, residual_grad_ref[...])
    start_stage(0, 0)
    fill(1, over_rows(grad_target_ref, by_line_ref, depth))
    start_stage(1, 0)
    fill(2, over_rows(grad_source_ref, by_side_ref, width * columns))
    start_stage(2, 0)
    end_stage(0, 0)
    end_stage(1, 0)
    end_core()
    end_stage(2, 0)
    reduce_step(0)
    end_stage(0, 1)
    end_stage(1, 1)
    reduce_step(1)
    end_stage(2, 1)
    end_lanes()
    end_stage(0, 2)
    reduce_step(2)
    end_stage(1, 2)
    end_stage(2, 2)
    end_return(0, 2)
    end_return(1, 2)
    for step in range(3, depth):
        reduce_step(step)
    end_return(2, 2)
    end_return(0, 1)
    end_return(1, 1)
    arrive(climbed, fallen, me, depth, width, sems)
    total = grad_target_ref[line] + climbed[line] + fallen[line]
    grad_features = features_grad_ref[...] + dot(target_weight_ref[...], total, HIGH)
    end_return(2, 1)
    grad_features_ref[...] = grad_features + dot(source_weight_ref[...], end_sides(), HIGH)
    end_return(0, 0)
    end_return(1, 0)
    end_return(2, 0)
    finish_reduce(work, climbed, fallen, me, depth, width, sems)


def outputs_kernel(
    output_in, features_in, weights_in, sums_in,
    output_ref, features_ref, source_ref, target_ref, vector_ref, bias_ref, residual_ref, gain_ref,
    shift_ref,
):
    heads, head_size = vector_ref.shape
    hidden = heads * head_size
    output_ref[...] = output_in[...]
    features_ref[...] = features_in[...].T
    residual_ref[...] = weights_in[0, :hidden, :].T
    target_ref[...] = weights_in[1, :hidden, :].T
    source_ref[...] = weights_in[2, :hidden, :].T
    sums = sums_in[...]
    for head in range(heads):
        vector_ref[head : head + 1, :] = sums[0:1, head * head_size : (head + 1) * head_size]
    bias_ref[...] = sums[1:2, :]
    gain_ref[...] = sums[2:3, :]
    shift_ref[...] = sums[3:4, :]


def list_chunks(chunks_ref, chunk_block, chunk_first, blocks, tile):
    def of_block(block, count):
        def one(chunk, count):
            chunk_block[count] = block
            chunk_first[count] = chunk * tile
            return count + 1

        return lax.fori_loop(0, chunks_ref[block], one, count)

    count = lax.fori_loop(0, blocks, of_block, jnp.int32(0))
    for extra in range(STAGES - 1):
        chunk_block[count + extra] = 0
        chunk_first[count + extra] = 1 << 20
    return count


def virtual_rows(bounds_ref, row_ref, turned_ref, block, first, tile):
    place = (iota((tile, tile), 1) + first).astype(F32)
    inside = (place >= bounds_ref[block, 0]) & (place < bounds_ref[block, 1])
    owner = jnp.where(inside, 1.0, 0.0).astype(BF16)
    rows = dot(row_ref[block], owner)
    base = (place[0:1] - rows[25:26] * 64.0 - rows[26:27]) * RANKS
    ranked = dot(turned_ref[block], owner)
    choice = [
        jnp.where(ranked == base + (r + 1), 1.0, 0.0).astype(BF16) for r in range(RANKS)
    ]
    return owner, rows[0:8] + rows[8:16] + rows[16:24], rows[24:25] - base, choice


def back_to_rows(parts, owner):
    return dot_lanes(jnp.concatenate(parts, 1), jnp.concatenate([owner, owner], 1))


def forward_kernel(
    chunks_ref, picks, turned_ref, bounds_ref, row_ref, target_ref, selfs_ref, source_ref, vector_ref,
    summed_ref, table_ref,
    chunk_block, chunk_first, totals, choice_in, target_in, rows_in, owner_in, values_in, logits_in,
    *, heads, columns, slots,
):
    depth, _, tile = summed_ref.shape
    pairs, hidden, wide = table_ref.shape
    wide = wide // 2
    vector = vector_ref[...]
    count = list_chunks(chunks_ref, chunk_block, chunk_first, pairs, tile)
    for pair in range(pairs):
        for slot in range(slots):
            both = source_ref[pair // depth * columns + picks[pair * slots + slot]]
            for part in range(2):
                place = part * wide + slot * tile
                table_ref[pair, :, place : place + tile] = both[:, part * tile : (part + 1) * tile]
    for ref in (summed_ref, totals, choice_in, target_in, rows_in, owner_in, values_in, logits_in):
        ref[...] = jnp.zeros_like(ref)

    def choose(index):
        block = chunk_block[index]
        owner, near, left, choice = virtual_rows(
            bounds_ref, row_ref, turned_ref, block, chunk_first[index], tile
        )
        for r in range(RANKS):
            choice_in[:, r * tile : (r + 1) * tile] = choice[r]
        target_in[...] = dot(
            target_ref[lax.rem(block, depth)], jnp.concatenate([owner, owner], 0)
        )
        rows_in[0, :8] = near
        rows_in[0, 8:] = jnp.broadcast_to(left, (8, tile))
        owner_in[0] = owner

    def score(index):
        choice = choice_in[...]
        values = dot(table_ref[chunk_block[index]], jnp.concatenate([choice, choice], 0))
        target = target_in[...]
        values_in[...] = values
        for r in range(RANKS):
            half = values[:, r * tile : (r + 1) * tile] + target
            active = half * jnp.tanh(half) + half
            logits_in[r] = head_rows(active * vector, heads)
        rows_in[1] = rows_in[0]
        owner_in[1] = owner_in[0]

    def gather_up(index):
        block = chunk_block[index]
        shift, left = rows_in[1, :heads], rows_in[1, 8:9]
        total = jnp.zeros((heads, tile), F32)
        summed = jnp.zeros((hidden, tile), F32)
        for r in range(RANKS):
            weight = jnp.where(left > r, jnp.exp(logits_in[r] - shift), 0.0)
            total = total + weight
            summed = summed + spread(weight, hidden) * values_in[:, r * tile : (r + 1) * tile]
        owner = owner_in[1]
        block = lax.rem(block, depth)
        summed_ref[block, :hidden] += back_to_rows(split(summed), owner)
        pad = jnp.zeros((heads, tile), F32)
        total = jnp.concatenate([pad, total, jnp.zeros((8, tile), F32)], 0)
        totals[block] += back_to_rows(split(total), owner)

    def step(index, carry):
        gather_up(jnp.maximum(index - 2, 0))
        score(jnp.maximum(index - 1, 0))
        choose(index)
        return carry

    lax.fori_loop(0, count + STAGES - 1, step, 0)
    summed_ref[...] = summed_ref[...] * 2.0
    for block in range(depth):
        summed_ref[block, hidden:] = selfs_ref[block] + totals[block, :8]
    over = jnp.where(totals[...] <= LARGEST, 0.0, 1.0)

    @pl.when(jnp.max(over) > 0.0)
    def _():
        def one(block, carry):
            summed_ref[block] = online_block(
                turned_ref, target_ref, table_ref, vector, depth, heads, block
            )
            return carry

        lax.fori_loop(0, depth, one, 0)


def online_block(turned_ref, target_ref, table_ref, vector, depth, heads, block):
    hidden, tile = vector.shape
    target = target_ref[block].astype(F32)
    target = target[:, :tile] + target[:, tile:]

    def of_pair(lane, carry):
        pair = lane * depth + block
        degree = jnp.max(turned_ref[pair].astype(F32), axis=0, keepdims=True)
        steps = (jnp.max(degree).astype(jnp.int32) + (RANKS - 1)) // RANKS

        def step(index, carry):
            top, total, summed = carry
            first = (index * RANKS).astype(F32)
            choice = jnp.concatenate(
                [
                    jnp.where(turned_ref[pair].astype(F32) == first + (r + 1), 1.0, 0.0).astype(BF16)
                    for r in range(RANKS)
                ],
                1,
            )
            values = dot(table_ref[pair], jnp.concatenate([choice, choice], 0))
            for r in range(RANKS):
                value = values[:, r * tile : (r + 1) * tile]
                half = value + target
                active = half * jnp.tanh(half) + half
                logits = jnp.where(first + r < degree, head_rows(active * vector, heads), NEGATIVE)
                new_top = jnp.maximum(top, logits)
                keep = jnp.exp(top - new_top)
                weight = jnp.exp(logits - new_top)
                total = total * keep + weight
                summed = summed * spread(keep, hidden) + spread(weight, hidden) * value
                top = new_top
            return top, total, summed

        return lax.fori_loop(0, steps, step, carry)

    zero = jnp.zeros((heads, tile), F32)
    top, total, summed = lax.fori_loop(
        0, turned_ref.shape[0] // depth, of_pair,
        (zero + NEGATIVE, zero, jnp.zeros((hidden, tile), F32)),
    )
    return jnp.concatenate([summed * 2.0, top, total], 0)


def backward_kernel(
    picks, chunks_ref, turned_ref, bounds_ref, row_ref, target_ref, grads_ref, own_target_ref,
    own_source_ref, table_ref, vector_ref,
    grad_target_ref, grad_source_ref, grad_vector_ref,
    chunk_block, chunk_first, collected, vector_sums, choice_in, target_in, grad_in, rows_in, owner_in,
    logits_in, products_in, active_in, slope_in, *, slots, heads, columns, width,
):
    depth, hidden, tile = grad_target_ref.shape
    pairs = turned_ref.shape[0]
    vector = vector_ref[...]
    half_vector = vector * 0.5
    count = list_chunks(chunks_ref, chunk_block, chunk_first, pairs, tile)
    for ref in (
        grad_target_ref, grad_source_ref, collected, vector_sums, choice_in, target_in, grad_in, rows_in,
        owner_in, logits_in, products_in, active_in, slope_in,
    ):
        ref[...] = jnp.zeros_like(ref)
    me = lax.axis_index("src")
    grad_target_ref[me // width] = own_target_ref[...]
    grad_source_ref[me % width * columns + lax.axis_index("dst")] = own_source_ref[...]

    def choose(index):
        block = chunk_block[index]
        owner, near, left, choice = virtual_rows(
            bounds_ref, row_ref, turned_ref, block, chunk_first[index], tile
        )
        for r in range(RANKS):
            choice_in[0, :, r * tile : (r + 1) * tile] = choice[r]
        twice = jnp.concatenate([owner, owner], 0)
        target_in[...] = dot(target_ref[lax.rem(block, depth)], twice)
        grad_in[0] = dot(grads_ref[lax.rem(block, depth)], twice)
        rows_in[0, :8] = near
        rows_in[0, 8:] = jnp.broadcast_to(left, (8, tile))
        owner_in[0] = owner

    def score(index):
        choice = choice_in[0]
        values = dot(table_ref[chunk_block[index]], jnp.concatenate([choice, choice], 0))
        target, grad = target_in[...], grad_in[0]
        for r in range(RANKS):
            value = values[:, r * tile : (r + 1) * tile]
            half = value + target
            risen = 1.0 + jnp.tanh(half)
            active = half * risen
            active_in[r] = active
            slope_in[r] = (risen + active * (2.0 - risen)) * half_vector
            logits_in[r] = head_rows(active * vector, heads)
            products_in[r] = head_rows(value * grad, heads)
        grad_in[1] = grad
        choice_in[1] = choice
        rows_in[1] = rows_in[0]
        owner_in[1] = owner_in[0]

    def gather_up(index):
        block = chunk_block[index]
        log_total, delta, left = rows_in[1, :heads], rows_in[1, heads : 2 * heads], rows_in[1, 8:9]
        grad = grad_in[1]
        grad_target = jnp.zeros((hidden, tile), F32)
        grad_vector = vector_sums[...]
        outward = []
        for r in range(RANKS):
            weight = jnp.where(left > r, jnp.exp(logits_in[r] - log_total), 0.0)
            grad_logit = spread(weight * (2.0 * products_in[r] - delta), hidden)
            grad_inner = grad_logit * slope_in[r]
            grad_target = grad_target + grad_inner
            grad_vector = grad_vector + grad_logit * active_in[r]
            outward.append(split(grad_inner + spread(weight, hidden) * grad))
        vector_sums[...] = grad_vector
        choice = choice_in[1]
        collected[block] += dot_lanes(
            jnp.concatenate([one for pair in zip(*outward) for one in pair], 1),
            jnp.concatenate([choice, choice], 1),
        )
        grad_target_ref[lax.rem(block, depth)] += back_to_rows(split(grad_target), owner_in[1])

    def step(index, carry):
        gather_up(jnp.maximum(index - 2, 0))
        score(jnp.maximum(index - 1, 0))
        choose(index)
        return carry

    lax.fori_loop(0, count + STAGES - 1, step, 0)
    for pair in range(pairs):
        for slot in range(slots):
            place = pair // depth * columns + picks[pair * slots + slot]
            grad_source_ref[place] += collected[pair, :, slot * tile : (slot + 1) * tile]
    grad_vector_ref[...] = dot_lanes(jnp.ones((8, tile), F32), vector_sums[...], HIGH)


def on_device(
    sources, columns, features, source_weight, target_weight, attention_vector, attention_bias, residual_weight,
    norm_gain, norm_shift, neighbours, slot_valid, edge_mask, node_count, out_cotangent,
):
    tile, hidden = features.shape
    heads, head_size = attention_vector.shape
    slots = neighbours.shape[-1]
    wide = slots * tile
    depth, width = grid_of(sources)
    picks, valid, edge_mask = neighbours[0, 0].T, slot_valid[0, 0].T, edge_mask[0, 0]
    counts = node_count.T
    dma = pltpu.SemaphoreType.DMA
    smem = pl.BlockSpec(memory_space=SMEM)
    whole = pl.BlockSpec(memory_space=VMEM)
    hbm = pl.BlockSpec(memory_space=pltpu.HBM)
    limit = min(32 + sources * columns // 4, 60) * 1024 * 1024

    def shaped(*shape):
        return jax.ShapeDtypeStruct(shape, F32)

    def halves(*shape):
        return jax.ShapeDtypeStruct(shape, BF16)

    def communicating(number):
        return pltpu.CompilerParams(
            collective_id=number, has_side_effects=True, vmem_limit_bytes=limit
        )

    many = max(columns - 1, 1)
    more = max(width - 1, 1)
    edge_mask_tiles = (width, depth, slots, tile, tile)
    (
        by_line, by_side, target_all, source_all, turned, info, bounds, self_rows, selfs, source_own,
        target_own, vector, chunks, pair_picks,
    ) = pl.pallas_call(
        functools.partial(gather_kernel, sources=sources, columns=columns, heads=heads),
        in_specs=[smem] * 3 + [whole] + [hbm] * 4,
        out_specs=[whole] * 12 + [smem] * 2,
        out_shape=[
            shaped(depth, tile, hidden), shaped(width * columns, tile, hidden),
            halves(depth, hidden, 2 * tile), halves(width * columns, hidden, 2 * tile),
            halves(sources, wide, tile), shaped(sources, 8, tile), shaped(sources, 2, tile, tile),
            halves(sources, 32, tile), shaped(depth, 8, tile), shaped(hidden, tile),
            shaped(hidden, tile), shaped(hidden, tile),
            jax.ShapeDtypeStruct((sources,), jnp.int32),
            jax.ShapeDtypeStruct((sources * slots,), jnp.int32),
        ],
        scratch_shapes=[
            VMEM(edge_mask_tiles, jnp.int32), VMEM((width, 2 * depth * slots, tile), F32),
            VMEM((more, 2 * depth * slots, tile), F32), VMEM((hidden, hidden), F32),
            VMEM((hidden, hidden), F32), VMEM((8, tile), F32), dma((4,)), dma((depth,)),
            *gather_semaphores(depth), dma((many + more,)), dma((width * columns,)),
            dma((more, many)), dma((more, depth)), dma((width, depth)), dma((more,)), dma((width,)),
            *small_semaphores(depth),
        ],
        compiler_params=communicating(0),
    )(*[pltpu.with_memory_space_constraint(one, pltpu.HBM) for one in (
        picks, valid, counts, attention_vector, features, edge_mask, source_weight, target_weight
    )])

    most = sources * (-(-wide // RANKS)) + STAGES
    lists = [SMEM((most,), jnp.int32), SMEM((most,), jnp.int32)]
    params = pltpu.CompilerParams(vmem_limit_bytes=limit)
    slot_rows = VMEM((2, 16, tile), F32)
    owners = VMEM((2, tile, tile), BF16)
    by_rank = VMEM((RANKS, heads, tile), F32)
    summed, table = pl.pallas_call(
        functools.partial(forward_kernel, heads=heads, columns=columns, slots=slots),
        in_specs=[smem] * 2 + [whole] * 7,
        out_specs=[whole] * 2,
        out_shape=[shaped(depth, hidden + 8, tile), halves(sources, hidden, 2 * wide)],
        scratch_shapes=[
            *lists, VMEM((depth, 16, tile), F32), VMEM((wide, RANKS * tile), BF16),
            VMEM((hidden, tile), F32), slot_rows, owners, VMEM((hidden, RANKS * tile), F32), by_rank,
        ],
        compiler_params=params,
    )(chunks, pair_picks, turned, bounds, self_rows, target_all, selfs, source_all, vector)

    (
        output, log_rows, grads, own_target, own_source, rows, residual_grad, features_grad,
    ) = pl.pallas_call(
        functools.partial(middle_kernel, sources=sources, heads=heads),
        in_specs=[smem] + [whole] * 11,
        out_specs=[whole] * 8,
        out_shape=[
            shaped(tile, hidden), halves(sources, 32, tile), halves(depth, hidden, 2 * tile),
            shaped(hidden, tile), shaped(hidden, tile), shaped(8, hidden),
            shaped(hidden, hidden), shaped(hidden, tile),
        ],
        scratch_shapes=[
            VMEM((depth, hidden, tile), F32), VMEM((depth, 8, tile), F32), VMEM((8, tile), F32),
            *small_semaphores(depth), *gather_semaphores(depth),
            *reduce_scratch(depth, hidden + 8, tile),
        ],
        compiler_params=communicating(1),
    )(
        counts, summed, features, source_own, target_own, info, residual_weight,
        vector, attention_bias.reshape(1, hidden), norm_gain.reshape(1, hidden),
        norm_shift.reshape(1, hidden), out_cotangent,
    )

    grad_targets, grad_sources, vector_grad = pl.pallas_call(
        functools.partial(backward_kernel, slots=slots, heads=heads, columns=columns, width=width),
        in_specs=[smem] * 2 + [whole] * 9,
        out_specs=[whole] * 3,
        out_shape=[
            shaped(depth, hidden, tile), shaped(width * columns, hidden, tile), shaped(8, hidden)
        ],
        scratch_shapes=[
            *lists, VMEM((sources, hidden, wide), F32), VMEM((hidden, tile), F32),
            VMEM((2, wide, RANKS * tile), BF16), VMEM((hidden, tile), F32),
            VMEM((2, hidden, tile), F32), slot_rows, owners, by_rank, by_rank,
            VMEM((RANKS, hidden, tile), F32), VMEM((RANKS, hidden, tile), F32),
        ],
        compiler_params=params,
    )(
        pair_picks, chunks, turned, bounds, log_rows, target_all, grads, own_target, own_source, table,
        vector,
    )

    step = 8 * sources * columns
    stacked = -(-hidden // step) * step
    across = columns // 2
    sizes = [2, across, sources]
    lengths = [stacked // 2, stacked // columns, stacked // columns // sources]

    def per_stage(make):
        return [make(max(size - 1, 1), length) for size, length in zip(sizes, lengths)]

    grad_features, weights, sums = pl.pallas_call(
        functools.partial(last_kernel, sources=sources, columns=columns),
        in_specs=[whole] * 10,
        out_specs=[whole] * 3,
        out_shape=[shaped(hidden, tile), shaped(3, stacked, hidden), shaped(8, hidden)],
        scratch_shapes=[
            VMEM((3, stacked, hidden), F32),
            per_stage(lambda n, length: VMEM((3, n, length, hidden), F32)),
            per_stage(lambda n, length: VMEM((n, 8, hidden), F32)),
            *[per_stage(lambda n, length: dma((3, n))) for _ in range(2)],
            *[per_stage(lambda n, length: dma((n,))) for _ in range(2)],
            *[per_stage(lambda n, length: dma((3, n))) for _ in range(2)],
            VMEM((width * across, hidden, tile), F32), VMEM((width * across, hidden, tile), F32),
            dma((width * across,)), dma((width * across,)),
            VMEM((more * across, hidden, tile), F32), VMEM((across, hidden, tile), F32),
            dma((more * across,)), dma((more * across,)),
            VMEM((max(across - 1, 1), hidden, tile), F32), dma((max(across - 1, 1),)),
            dma((max(across - 1, 1),)),
            *reduce_scratch(depth, hidden, tile),
        ],
        compiler_params=communicating(2),
    )(
        grad_targets, grad_sources, vector_grad, rows, by_line, by_side, residual_grad,
        features_grad, source_weight, target_weight,
    )

    line = shaped(1, hidden)
    square = shaped(hidden, hidden)
    output, *rest = pl.pallas_call(
        outputs_kernel,
        in_specs=[whole] * 4,
        out_specs=[whole] * 9,
        out_shape=[
            shaped(tile, hidden), shaped(tile, hidden), square, square, shaped(heads, head_size),
            line, square, line, line,
        ],
        compiler_params=pltpu.CompilerParams(vmem_limit_bytes=limit),
    )(output, grad_features, weights, sums)
    return (output, *[one.reshape(hidden) if one.shape[0] == 1 else one for one in rest])


def solution(mesh):
    rows = P(("src", "dst"), None)
    placed = (
        rows, P(), P(), P(), P(), P(), P(), P(),
        P("src", "dst", None, None), P("src", "dst", None, None),
        P("src", "dst", None, None, None, None), P(), rows,
    )
    return jax.shard_map(
        functools.partial(on_device, mesh.shape["src"], mesh.shape["dst"]),
        mesh=mesh, in_specs=placed,
        out_specs=(rows, rows, P(), P(), P(), P(), P(), P(), P()), check_vma=False,
    )
```

```python
import functools

import jax
import jax.numpy as jnp
from jax import lax
from jax.experimental import pallas as pl
from jax.experimental.pallas import tpu as pltpu
from jax.sharding import PartitionSpec as P

HIGH = lax.Precision.HIGHEST
NEGATIVE = -1e30
EPSILON = 1e-05
RANKS = 4
STAGES = 3
LARGEST = 1e26
F32 = jnp.float32
BF16 = jnp.bfloat16
VMEM = pltpu.VMEM
SMEM = pltpu.SMEM


def iota(shape, axis):
    return lax.broadcasted_iota(jnp.int32, shape, axis)


def split(values):
    high = values.astype(BF16)
    return high, (values - high.astype(F32)).astype(BF16)


def dot(left, right, precision=None):
    return jnp.dot(left, right, preferred_element_type=F32, precision=precision)


def dot_lanes(left, right, precision=None):
    return lax.dot_general(
        left, right, (((1,), (1,)), ((), ())), preferred_element_type=F32, precision=precision
    )


def split3(values):
    high, rest = split_off(values)
    middle, rest = split_off(rest)
    return high, middle, rest.astype(BF16)


def split_off(values):
    high = values.astype(BF16)
    return high, values - high.astype(F32)


def head_rows(values, heads):
    size = values.shape[0] // heads
    return jnp.concatenate(
        [jnp.sum(values[h * size : (h + 1) * size], axis=0, keepdims=True) for h in range(heads)], 0
    )


def spread(rows, hidden):
    heads, wide = rows.shape
    return jnp.concatenate(
        [jnp.broadcast_to(rows[h : h + 1], (hidden // heads, wide)) for h in range(heads)], 0
    )


def upright(row, tile):
    return jnp.broadcast_to(row, (tile, row.shape[1])).T


def row_table(values, info):
    return jnp.concatenate([*(part.astype(F32) for part in split3(values)), info], 0).astype(BF16)


def build_ranks(mask_ref, counts, rows, tile, slots):
    parts = []
    for slot in range(slots):
        shape = (tile, tile)
        near = iota(shape, 1).astype(F32) < counts[slot : slot + 1]
        live = (mask_ref[slot] != 0) & near & (iota(shape, 0) < rows)
        parts.append(live.astype(F32).T)
    live = jnp.concatenate(parts, 0)
    wide = slots * tile
    before = (iota((wide, wide), 1) <= iota((wide, wide), 0)).astype(F32).astype(BF16)
    ranks = live * dot(before, live.astype(BF16))
    degree = dot(jnp.ones((8, wide), BF16), live.astype(BF16))
    pieces = jnp.floor((degree + (RANKS - 1)) * (1.0 / RANKS))
    earlier = (iota((tile, tile), 0) < iota((tile, tile), 1)).astype(F32).astype(BF16)
    start = dot(pieces.astype(BF16), earlier)
    end = start + pieces
    coarse = jnp.floor(start * (1.0 / 64.0))
    row = iota((8, tile), 0)
    info = jnp.where(row == 0, degree, jnp.where(row == 1, coarse, start - 64.0 * coarse))
    chunks = (jnp.max(end).astype(jnp.int32) + (tile - 1)) // tile
    return ranks.astype(BF16), info, upright(start[0:1], tile), upright(end[0:1], tile), chunks


MESH = pl.DeviceIdType.MESH


def grid_of(sources):
    depth = 4 if sources % 4 == 0 else 1
    return depth, sources // depth


def greet(peers):
    barrier = pltpu.get_barrier_semaphore()
    for peer in peers:
        pl.semaphore_signal(barrier, inc=1, device_id=peer, device_id_type=MESH)
    pl.semaphore_wait(barrier, len(peers))


def remote(source, target, send, recv, peer):
    return pltpu.make_async_remote_copy(
        src_ref=source, dst_ref=target, send_sem=send, recv_sem=recv,
        device_id=peer, device_id_type=MESH,
    )


def line_peers(me, depth, width):
    line, lane = me // width, me % width
    return [{"src": lax.rem(line + k, depth) * width + lane} for k in range(1, depth)]


def lane_peers(me, width):
    line, lane = me // width, me % width
    return [{"src": line * width + lax.rem(lane + k, width)} for k in range(1, width)]


def src_peers(me, sources):
    return [{"src": lax.rem(me + k, sources)} for k in range(1, sources)]


def dst_peers(column, columns):
    return [{"dst": lax.rem(column + k, columns)} for k in range(1, columns)]


def start_reduce(blocks, landed, me, depth, width, send, recv, steps):
    line, lane = me // width, me % width
    for step in steps:
        far = jnp.where(line < depth // 2, depth - 1 - step, step)
        far = jnp.where(
            jnp.where(line < depth // 2, far <= line, far >= line),
            jnp.where(line < depth // 2, far - 1, far + 1), far,
        )
        remote(
            blocks.at[far], landed.at[line], send.at[far], recv.at[line], {"src": far * width + lane}
        ).start()


def wait_reduce(blocks, landed, me, depth, width, send, recv):
    for k, peer in enumerate(line_peers(me, depth, width)):
        other = lax.rem(me // width + k + 1, depth)
        remote(blocks.at[other], landed.at[other], send.at[other], recv.at[other], peer).wait_recv()


def finish_reduce(blocks, landed, me, depth, width, send, recv):
    for k, peer in enumerate(line_peers(me, depth, width)):
        other = lax.rem(me // width + k + 1, depth)
        remote(blocks.at[other], landed.at[other], send.at[other], recv.at[other], peer).wait_send()


def reduce_scratch(depth, rows, hidden):
    dma = pltpu.SemaphoreType.DMA
    return [VMEM((depth, rows, hidden), F32), dma((depth,)), dma((depth,))]


def start_all(own, slots, me, depth, width, send, recv):
    for k, peer in enumerate(line_peers(me, depth, width)):
        remote(own, slots.at[me // width], send.at[k], recv.at[me // width], peer).start()


def wait_all(own, slots, me, depth, width, send, recv, use=None):
    for k, peer in enumerate(line_peers(me, depth, width)):
        other = lax.rem(me // width + k + 1, depth)
        remote(own, slots.at[other], send.at[k], recv.at[other], peer).wait_recv()
        if use is not None:
            use(other)


def finish_all(own, slots, me, depth, width, send, recv):
    for k, peer in enumerate(line_peers(me, depth, width)):
        remote(own, slots.at[me // width], send.at[k], recv.at[me // width], peer).wait_send()


def line_semaphores(depth):
    return [pltpu.SemaphoreType.DMA((max(depth - 1, 1),)), pltpu.SemaphoreType.DMA((depth,))]


def gather_kernel(
    picks_in, valid_in, counts_in, vector_in, features_ref, mask_ref, source_weight_ref,
    target_weight_ref, by_line_ref, by_side_ref, target_ref, source_ref, turned_ref, info_ref, bounds_ref, row_ref,
    selfs_ref, own_source_ref, own_target_ref, vector_out_ref, real_ref, plan_ref,
    picks, valid, counts, vector_ref,
    masks, tiles, own_tiles, source_weight, target_weight, own_self, local, own_masks,
    send, recv, side_send, side_recv, pass_send, mask_send, mask_recv, tile_send, tile_recv,
    self_send, self_recv, *, sources, columns, heads,
):
    me, column = lax.axis_index("src"), lax.axis_index("dst")
    depth, width = grid_of(sources)
    line, lane = me // width, me % width
    _, slots, tile, _ = mask_ref.shape
    hidden = features_ref.shape[1]
    sideways, lanes = dst_peers(column, columns), lane_peers(me, width)
    here = lane * columns + column
    loads = [
        pltpu.make_async_copy(one, other, local.at[index])
        for index, (one, other) in enumerate(
            (
                (features_ref, by_line_ref.at[line]),
                (features_ref, by_side_ref.at[here]),
                (source_weight_ref, source_weight),
                (target_weight_ref, target_weight),
                (vector_in, vector_ref),
                (picks_in, picks),
                (valid_in, valid),
                (counts_in, counts),
            )
        )
    ]
    mask_loads = [
        pltpu.make_async_copy(mask_ref.at[far * width + lane], masks.at[lane, far], own_masks.at[far])
        for far in range(depth)
    ]
    for load in [*loads, *mask_loads]:
        load.start()

    def tile_of(other):
        shape = (2 * depth * slots, tile)
        row = iota(shape, 0)
        total = jnp.zeros(shape, F32)
        for far in range(depth):
            block = far * width + other
            for slot in range(slots):
                pick = picks[slot, block]
                have = valid[slot, block] * counts[pick, me]
                place = far * slots + slot
                total = jnp.where(row == place, have.astype(F32), total)
                total = jnp.where(row == place + depth * slots, pick.astype(F32), total)
        return total

    greet([*line_peers(me, depth, width), *lanes, *sideways])

    start_all(features_ref, by_line_ref, me, depth, width, send, recv)
    own_slot = by_side_ref.at[here]
    for k, peer in enumerate([*sideways, *lanes]):
        remote(features_ref, own_slot, side_send.at[k], side_recv.at[here], peer).start()
    for load in loads[5:]:
        load.wait()
    tiles[lane] = tile_of(lane)
    for k, peer in enumerate(lanes):
        other = lax.rem(lane + k + 1, width)
        own_tiles[k] = tile_of(other)
        remote(own_tiles.at[k], tiles.at[lane], tile_send.at[k], tile_recv.at[lane], peer).start()
        for far in range(depth):
            remote(
                mask_ref.at[far * width + other], masks.at[lane, far], mask_send.at[k, far],
                mask_recv.at[lane, far], peer,
            ).start()

    def keep(to_ref, index, values):
        high, low = split(values * 0.5)
        to_ref[index, :, :tile] = high
        to_ref[index, :, tile:] = low

    def project_target(index):
        keep(target_ref, index, dot_lanes(target_weight[...], by_line_ref[index], HIGH))

    def project_source(index):
        keep(source_ref, index, dot_lanes(source_weight[...], by_side_ref[index], HIGH))

    def rank(other, far):
        pair = other * depth + far
        tile_here = tiles[other]
        ranks, info, start, end, chunks = build_ranks(
            masks.at[other, far], tile_here[far * slots : (far + 1) * slots],
            counts[column, far * width + lane], tile, slots,
        )
        turned_ref[pair] = ranks
        info_ref[pair] = info
        bounds_ref[pair, 0] = start
        bounds_ref[pair, 1] = end
        plan_ref[pair] = chunks
        for slot in range(slots):
            place = depth * slots + far * slots + slot
            pick = jnp.max(tile_here[place : place + 1])
            plan_ref[sources + pair * slots + slot] = pick.astype(jnp.int32)

    for load in loads[:5]:
        load.wait()
    real_ref[...] = (iota((8, tile), 1) < counts[column, me]).astype(F32)
    source_weight[...] = source_weight[...].T
    target_weight[...] = target_weight[...].T
    row = jnp.concatenate([vector_ref[head : head + 1, :] for head in range(heads)], 1)
    vector = upright(row, tile)
    vector_out_ref[...] = vector
    own = by_line_ref[line]
    own_source = dot_lanes(source_weight[...], own, HIGH)
    own_target = dot_lanes(target_weight[...], own, HIGH)
    own_source_ref[...] = own_source
    own_target_ref[...] = own_target
    half = 0.5 * (own_source + own_target)
    active = (half * jnp.tanh(half) + half) * vector
    own_self[...] = jnp.concatenate(
        [head_rows(active, heads), jnp.zeros((8 - heads, tile), F32)], 0
    )
    selfs_ref[line] = own_self[...]
    start_all(own_self, selfs_ref, me, depth, width, self_send, self_recv)
    keep(source_ref, here, own_source)
    keep(target_ref, line, own_target)

    def pass_sideways():
        for k in range(1, width):
            index = lax.rem(lane + k, width) * columns + column
            piece = by_side_ref.at[index]
            remote(piece, piece, side_send.at[0], side_recv.at[index], {"dst": column}).wait_recv()
            for j, peer in enumerate(sideways):
                remote(piece, piece, pass_send.at[k - 1, j], side_recv.at[index], peer).start()

    def take_side(index):
        piece = by_side_ref.at[index]
        remote(piece, piece, side_send.at[0], side_recv.at[index], {"dst": column}).wait_recv()
        project_source(index)

    def rank_other(k, far):
        other = lax.rem(lane + k, width)
        mask = masks.at[other, far]
        remote(mask, mask, mask_send.at[0, 0], mask_recv.at[other, far], {"dst": column}).wait_recv()
        rank(other, far)

    def take_line(k):
        if k >= depth:
            return
        other = lax.rem(line + k, depth)
        piece = by_line_ref.at[other]
        remote(piece, piece, send.at[0], recv.at[other], {"dst": column}).wait_recv()
        project_target(other)

    for load in mask_loads:
        load.wait()
    rank(lane, 0)
    pass_sideways()
    for k in range(1, width):
        project_source(lax.rem(lane + k, width) * columns + column)
    for far in range(1, depth // 2):
        rank(lane, far)
    for k in range(1, columns):
        take_side(lane * columns + lax.rem(column + k, columns))
    for k in range(1, width):
        other = lax.rem(lane + k, width)
        tile_slot = tiles.at[other]
        remote(
            tile_slot, tile_slot, tile_send.at[0], tile_recv.at[other], {"dst": column}
        ).wait_recv()
        rank_other(k, 0)
    for far in range(max(depth // 2, 1), depth):
        rank(lane, far)
    for k in range(1, depth):
        take_line(k)
    for k in range(1, width):
        for far in range(1, depth // 2):
            rank_other(k, far)
    for k in range(1, width):
        other = lax.rem(lane + k, width)
        for j in range(1, columns):
            take_side(other * columns + lax.rem(column + j, columns))
    for k in range(1, width):
        for far in range(max(depth // 2, 1), depth):
            rank_other(k, far)
    wait_all(own_self, selfs_ref, me, depth, width, self_send, self_recv)
    for pair in range(sources):
        row_ref[pair] = row_table(selfs_ref[pair % depth], info_ref[pair])
    finish_all(features_ref, by_line_ref, me, depth, width, send, recv)
    finish_all(own_self, selfs_ref, me, depth, width, self_send, self_recv)
    for k, peer in enumerate([*sideways, *lanes]):
        remote(features_ref, own_slot, side_send.at[k], side_recv.at[here], peer).wait_send()
    for k, peer in enumerate(lanes):
        for j in range(columns - 1):
            remote(own_slot, own_slot, pass_send.at[k, j], side_recv.at[here], peer).wait_send()
        remote(own_tiles.at[k], tiles.at[lane], tile_send.at[k], tile_recv.at[lane], peer).wait_send()
        for far in range(depth):
            remote(
                mask_ref.at[far], masks.at[lane, far], mask_send.at[k, far], mask_recv.at[lane, far], peer
            ).wait_send()


def middle_kernel(
    real_ref, summed_ref, features_ref, source_ref, target_ref, info_ref,
    residual_weight_ref, vector_ref, bias_ref, gain_ref, shift_ref, cotangent_ref,
    output_ref, row_ref, grads_ref, own_target_ref, own_source_ref, rows_ref,
    residual_grad_ref, features_grad_ref,
    pieces, small, own_small, small_send, small_recv,
    gather_send, gather_recv, landed, reduce_send, reduce_recv, *, sources, heads,
):
    me = lax.axis_index("src")
    depth, width = grid_of(sources)
    line = me // width
    hidden, tile = source_ref.shape
    greet(line_peers(me, depth, width))

    def merge(parts):
        tops = [part[hidden : hidden + heads] for part in parts]
        top = functools.reduce(jnp.maximum, tops)
        keep = [jnp.exp(one - top) for one in tops]
        summed = sum(part[:hidden] * spread(one, hidden) for part, one in zip(parts, keep))
        total = sum(part[hidden + heads :] * one for part, one in zip(parts, keep))
        return jnp.concatenate([summed, top, total], 0)

    start_reduce(summed_ref, landed, me, depth, width, reduce_send, reduce_recv, range(depth - 1))
    source = source_ref[...]
    features = features_ref[...]
    vector = vector_ref[...]
    half = 0.5 * (source + target_ref[...])
    risen = 1.0 + jnp.tanh(half)
    active = half * risen
    slope = (risen + active * (2.0 - risen)) * (0.5 * vector)
    self_logit = head_rows(active * vector, heads)
    residual = dot_lanes(residual_weight_ref[...].T, features, HIGH) + upright(bias_ref[...], tile)
    gain = upright(gain_ref[...], tile)
    shift = upright(shift_ref[...], tile)
    real = jnp.broadcast_to(real_ref[0:1], (hidden, tile))
    cotangent = cotangent_ref[...].T * real
    landed[line] = summed_ref[line]
    wait_reduce(summed_ref, landed, me, depth, width, reduce_send, reduce_recv)
    remote_part = merge([landed[index] for index in range(depth)])
    remote_top = remote_part[hidden : hidden + heads]
    remote_total = remote_part[hidden + heads :]
    top = jnp.maximum(remote_top, self_logit)
    keep_remote = jnp.exp(remote_top - top)
    self_weight = jnp.exp(self_logit - top)
    denominator = remote_total * keep_remote + self_weight
    log_total = top + jnp.log(denominator)
    inverse = 1.0 / denominator
    self_alpha = spread(self_weight * inverse, hidden)
    keep_remote = spread(keep_remote * inverse, hidden)
    mixed = remote_part[:hidden] * keep_remote + source * self_alpha + residual

    def mean(values):
        return jnp.sum(values, axis=0, keepdims=True) * (1.0 / hidden)

    center = mixed - mean(mixed)
    scale = lax.rsqrt(mean(center * center) + EPSILON)
    unit = center * scale
    normed = unit * gain + shift
    below = jnp.exp(jnp.minimum(normed, 0.0))
    grad_normed = cotangent * jnp.where(normed > 0, 1.0, below)
    grad_unit = grad_normed * gain
    grad_mixed = scale * (grad_unit - mean(grad_unit) - unit * mean(grad_unit * unit))
    pieces[line] = grad_mixed
    own = pieces.at[line]
    start_all(own, pieces, me, depth, width, gather_send, gather_recv)
    delta = head_rows(grad_mixed * (mixed - residual), heads)
    own_small[...] = jnp.concatenate([log_total, delta], 0)
    small[line] = own_small[...]
    start_all(own_small, small, me, depth, width, small_send, small_recv)

    def expand(index):
        high, low = split(pieces[index])
        grads_ref[index, :, :tile] = high
        grads_ref[index, :, tile:] = low

    expand(line)
    products = head_rows(grad_mixed * source, heads)
    grad_logit = self_alpha * spread(products - delta, hidden)
    grad_inner = grad_logit * slope
    own_target_ref[...] = grad_inner
    own_source_ref[...] = self_alpha * grad_mixed + grad_inner
    output_ref[...] = (jnp.where(normed > 0, normed, below - 1.0) * real).T
    for index, values in enumerate(
        (grad_logit * active, grad_mixed, grad_normed * unit, grad_normed)
    ):
        rows_ref[index : index + 1, :] = dot_lanes(jnp.ones((8, tile), F32), values, HIGH)[0:1]
    rows_ref[4:, :] = jnp.zeros((4, hidden), F32)
    residual_grad_ref[...] = dot(grad_mixed, features, HIGH)
    features_grad_ref[...] = dot(residual_weight_ref[...], grad_mixed, HIGH)
    wait_all(own_small, small, me, depth, width, small_send, small_recv)
    for pair in range(sources):
        row_ref[pair] = row_table(small[pair % depth], info_ref[pair])
    wait_all(own, pieces, me, depth, width, gather_send, gather_recv, expand)
    finish_all(own, pieces, me, depth, width, gather_send, gather_recv)
    finish_reduce(summed_ref, landed, me, depth, width, reduce_send, reduce_recv)
    finish_all(own_small, small, me, depth, width, small_send, small_recv)


def return_stages(me, column, sources, columns):
    across = columns // 2
    half, core = column // 2, column % 2
    return [
        (2, core, lambda at: {"dst": half * 2 + at}),
        (across, half, lambda at: {"dst": at * 2 + core}),
        (sources, me, lambda at: {"src": at}),
    ]


def last_kernel(
    grad_target_ref, grad_source_ref, vector_grad_ref, rows_ref, by_line_ref, by_side_ref,
    residual_grad_ref, features_grad_ref, source_weight_ref, target_weight_ref,
    grad_features_ref, pair_ref, single_ref, sums_ref,
    partial, parts, sums_in, part_send, part_recv, sum_send, sum_recv, full_send, full_recv,
    core_in, core_sum, core_send, core_recv, lane_in, lane_sum, lane_send, lane_recv,
    side_in, side_send, side_recv, landed, reduce_send, reduce_recv, *, sources, columns,
):
    me, column = lax.axis_index("src"), lax.axis_index("dst")
    depth, width = grid_of(sources)
    line, lane = me // width, me % width
    hidden, tile = features_grad_ref.shape
    weights = [pair_ref, single_ref]
    rows = single_ref.shape[0]
    stages = return_stages(me, column, sources, columns)
    greet([*src_peers(me, sources), *dst_peers(column, columns)])

    across, half, core = columns // 2, column // 2, column % 2
    lanes = lane_peers(me, width)

    def core_copy(other, side):
        place = other * across + side
        return remote(
            grad_source_ref.at[other * columns + side * 2 + 1 - core], core_in.at[place],
            core_send.at[place], core_recv.at[place], {"dst": half * 2 + 1 - core},
        )

    def lane_copy(k, side):
        other = lax.rem(lane + k + 1, width)
        place = k * across + side
        return remote(
            core_sum.at[other * across + side], lane_in.at[place], lane_send.at[place],
            lane_recv.at[place], lanes[k],
        )

    def side_copy(k):
        side = lax.rem(half + k, across)
        return remote(
            lane_sum.at[side], side_in.at[k - 1], side_send.at[k - 1], side_recv.at[k - 1],
            {"dst": side * 2 + core},
        )

    def end_core():
        for other in range(width):
            for side in range(across):
                core_copy(other, side).wait()
                place = other * across + side
                core_sum[place] = (
                    grad_source_ref[other * columns + side * 2 + core] + core_in[place]
                )
        for k in range(width - 1):
            for side in range(across):
                lane_copy(k, side).start()

    def end_lanes():
        for side in range(across):
            total = core_sum[lane * across + side]
            for k in range(width - 1):
                lane_copy(k, side).wait()
                total = total + lane_in[k * across + side]
            lane_sum[side] = total
        for k in range(1, across):
            side_copy(k).start()

    def end_sides():
        total = lane_sum[half]
        for k in range(1, across):
            side_copy(k).wait()
            total = total + side_in[k - 1]
        return total

    def send_targets(steps):
        start_reduce(
            grad_target_ref, landed, me, depth, width, reduce_send, reduce_recv, steps
        )

    send_targets(range(min(1, depth - 1)))
    for other in range(width):
        for side in range(across):
            core_copy(other, side).start()

    def over_rows(grad_ref, features_ref, count):
        total = jnp.zeros((hidden, hidden), F32)
        for index in range(count):
            high, low = split(grad_ref[index])
            large, small = split(features_ref[index])
            total = total + dot(
                jnp.concatenate([high, low, high], 1), jnp.concatenate([large, large, small], 0)
            )
        return total

    def fill(number, begin, values):
        partial[number][begin : begin + hidden, :] = values
        if rows > hidden:
            partial[number][begin + hidden : begin + rows, :] = jnp.zeros((rows - hidden, hidden), F32)

    numbers = range(len(weights))
    lengths, offsets = [], []
    for number in numbers:
        height = partial[number].shape[0]
        quarter = height // columns
        begin = pl.multiple_of(core * (height // 2) + half * quarter, 8)
        lengths.append([height, height // 2, quarter, quarter // sources])
        offsets.append([
            0, core * (height // 2), begin, pl.multiple_of(begin + me * (quarter // sources), 8)
        ])

    def group_copies(number):
        height, _, quarter, _ = lengths[number]
        for k, peer in enumerate(dst_peers(column, columns)):
            other = lax.rem(column + k + 1, columns)
            begin = pl.multiple_of(other % 2 * (height // 2) + other // 2 * quarter, 8)
            yield remote(
                partial[number].at[pl.ds(begin, quarter), :], parts[number][0].at[k],
                part_send[0].at[number, k], part_recv[0].at[number, k], peer,
            )
            if number == 0:
                yield remote(
                    sums_ref, sums_in[0].at[k], sum_send[0].at[k], sum_recv[0].at[k], peer
                )

    def line_copies(number):
        length = lengths[number][3]
        for k, peer in enumerate(src_peers(me, sources)):
            other = lax.rem(me + k + 1, sources)
            begin = pl.multiple_of(offsets[number][2] + other * length, 8)
            yield remote(
                partial[number].at[pl.ds(begin, length), :], parts[number][1].at[k],
                part_send[1].at[number, k], part_recv[1].at[number, k], peer,
            )
            if number == 0:
                yield remote(
                    sums_ref, sums_in[1].at[k], sum_send[1].at[k], sum_recv[1].at[k], peer
                )

    def start_group(number):
        for copy in group_copies(number):
            copy.start()

    def add_up(number, copies, index, into):
        for copy in copies:
            copy.wait()
        own = pl.ds(offsets[number][index + 2], lengths[number][index + 2])
        total = partial[number][own, :]
        for k in range(parts[number][index].shape[0]):
            total = total + parts[number][index][k]
        into[own, :] = total
        if number == 0:
            sums = sums_ref[...]
            for k in range(sums_in[index].shape[0]):
                sums = sums + sums_in[index][k]
            sums_ref[...] = sums

    def end_group(number):
        add_up(number, group_copies(number), 0, partial[number])
        for copy in line_copies(number):
            copy.start()

    def end_line(number):
        add_up(number, line_copies(number), 1, weights[number])
        start_return(number, 2)

    def return_copies(number, index, waiting):
        size, place, peer_at = stages[index]
        part = lengths[number][index + 1]
        for k in range(1, size):
            at = lax.rem(place + (size - k if waiting else 0), size)
            start = pl.multiple_of(offsets[number][index] + at * part, 8)
            segment = weights[number].at[pl.ds(start, part), :]
            yield remote(
                segment, segment, full_send[index].at[number, k - 1],
                full_recv[index].at[number, k - 1], peer_at(lax.rem(place + k, size)),
            )

    def start_return(number, index):
        for copy in return_copies(number, index, False):
            copy.start()

    def end_return(number, index):
        for copy in return_copies(number, index, True):
            copy.wait()
        if index > 0:
            start_return(number, index - 1)

    sums = rows_ref[...]
    first_row = (iota(sums.shape, 0) == 0).astype(F32)
    sums_ref[...] = sums + first_row * vector_grad_ref[...]
    fill(0, 0, residual_grad_ref[...])
    fill(0, rows, over_rows(grad_target_ref, by_line_ref, depth))
    start_group(0)
    fill(1, 0, over_rows(grad_source_ref, by_side_ref, width * columns))
    start_group(1)
    end_core()
    for number in numbers:
        end_group(number)
    end_lanes()
    for number in numbers:
        end_line(number)
    send_targets(range(1, depth - 1))
    for number in numbers:
        end_return(number, 2)
    end_return(0, 1)
    landed[line] = grad_target_ref[line]
    wait_reduce(grad_target_ref, landed, me, depth, width, reduce_send, reduce_recv)
    total = sum(landed[index] for index in range(depth))
    grad_features = features_grad_ref[...] + dot(target_weight_ref[...], total, HIGH)
    end_return(1, 1)
    grad_features_ref[...] = grad_features + dot(source_weight_ref[...], end_sides(), HIGH)
    for number in numbers:
        end_return(number, 0)
    finish_reduce(grad_target_ref, landed, me, depth, width, reduce_send, reduce_recv)


def outputs_kernel(
    output_in, features_in, pair_in, single_in, sums_in,
    output_ref, features_ref, source_ref, target_ref, vector_ref, bias_ref, residual_ref, gain_ref,
    shift_ref,
):
    heads, head_size = vector_ref.shape
    hidden = heads * head_size
    output_ref[...] = output_in[...]
    features_ref[...] = features_in[...].T
    rows = single_in.shape[0]
    residual_ref[...] = pair_in[:hidden, :].T
    target_ref[...] = pair_in[rows : rows + hidden, :].T
    source_ref[...] = single_in[:hidden, :].T
    sums = sums_in[...]
    for head in range(heads):
        vector_ref[head : head + 1, :] = sums[0:1, head * head_size : (head + 1) * head_size]
    bias_ref[...] = sums[1:2, :]
    gain_ref[...] = sums[2:3, :]
    shift_ref[...] = sums[3:4, :]


def list_chunks(chunks_ref, chunk_block, chunk_first, blocks, tile):
    def of_block(block, count):
        def one(chunk, count):
            chunk_block[count] = block
            chunk_first[count] = chunk * tile
            return count + 1

        return lax.fori_loop(0, chunks_ref[block], one, count)

    count = lax.fori_loop(0, blocks, of_block, jnp.int32(0))
    for extra in range(STAGES - 1):
        chunk_block[count + extra] = 0
        chunk_first[count + extra] = 1 << 20
    return count


def virtual_rows(bounds_ref, row_ref, turned_ref, tables, block, first, tile):
    place = (iota((tile, tile), 1) + first).astype(F32)
    inside = (place >= bounds_ref[block, 0]) & (place < bounds_ref[block, 1])
    owner = jnp.where(inside, 1.0, 0.0).astype(BF16)
    wide = turned_ref.shape[1]
    parts = [table[:, part * tile : (part + 1) * tile] for table in tables for part in range(2)]
    taken = dot(jnp.concatenate([turned_ref[block], row_ref[block], *parts], 0), owner)
    ranked, rows = taken[:wide], taken[wide : wide + 32]
    columns, at = [], wide + 32
    for table in tables:
        height = table.shape[0]
        columns.append(taken[at : at + height] + taken[at + height : at + 2 * height])
        at = at + 2 * height
    base = (place[0:1] - rows[25:26] * 64.0 - rows[26:27]) * RANKS
    choice = [
        jnp.where(ranked == base + (r + 1), 1.0, 0.0).astype(BF16) for r in range(RANKS)
    ]
    return owner, rows[0:8] + rows[8:16] + rows[16:24], rows[24:25] - base, choice, columns


def by_parts(product, high, low, right):
    both = product(jnp.concatenate([high, low], 0), right)
    return both[: high.shape[0]] + both[high.shape[0] :]


def forward_kernel(
    plan_in, turned_ref, bounds_ref, row_ref, target_ref, selfs_ref, source_ref, vector_ref,
    summed_ref, table_ref, logits_ref,
    plan, plan_sem, chunk_block, chunk_first, totals, choice_in, target_in, rows_in, owner_in, values_in,
    *, heads, columns, slots,
):
    depth, _, tile = summed_ref.shape
    pairs, hidden, _ = table_ref.shape
    hidden = hidden // 2
    load = pltpu.make_async_copy(plan_in, plan, plan_sem)
    load.start()
    vector = vector_ref[...]
    logits_ref[0] = jnp.zeros(logits_ref.shape[1:], F32)
    for ref in (summed_ref, totals, choice_in, target_in, rows_in, owner_in, values_in):
        ref[...] = jnp.zeros_like(ref)
    load.wait()
    count = list_chunks(plan, chunk_block, chunk_first, pairs, tile)
    for pair in range(pairs):
        for slot in range(slots):
            both = source_ref[pair // depth * columns + plan[pairs + pair * slots + slot]]
            for part in range(2):
                table_ref[
                    pair, part * hidden : (part + 1) * hidden, slot * tile : (slot + 1) * tile
                ] = both[:, part * tile : (part + 1) * tile]

    def choose(index):
        block = chunk_block[index]
        owner, near, left, choice, columns = virtual_rows(
            bounds_ref, row_ref, turned_ref, [target_ref[lax.rem(block, depth)]], block,
            chunk_first[index], tile,
        )
        for r in range(RANKS):
            choice_in[:, r * tile : (r + 1) * tile] = choice[r]
        target_in[...] = columns[0]
        rows_in[0, :8] = near
        rows_in[0, 8:] = jnp.broadcast_to(left, (8, tile))
        owner_in[0] = owner

    def score(index):
        both = dot(table_ref[chunk_block[index]], choice_in[...])
        values = both[:hidden] + both[hidden:]
        target = target_in[...]
        values_in[...] = values
        for r in range(RANKS):
            half = values[:, r * tile : (r + 1) * tile] + target
            active = half * jnp.tanh(half) + half
            logits_ref[index, r] = head_rows(active * vector, heads)
        rows_in[1] = rows_in[0]
        owner_in[1] = owner_in[0]

    def gather_up(index):
        block = chunk_block[index]
        shift, left = rows_in[1, :heads], rows_in[1, 8:9]
        total = jnp.zeros((heads, tile), F32)
        summed = jnp.zeros((hidden, tile), F32)
        for r in range(RANKS):
            weight = jnp.where(left > r, jnp.exp(logits_ref[index, r] - shift), 0.0)
            total = total + weight
            summed = summed + spread(weight, hidden) * values_in[:, r * tile : (r + 1) * tile]
        owner = owner_in[1]
        block = lax.rem(block, depth)
        pad = jnp.zeros((heads, tile), F32)
        both = jnp.concatenate([summed, pad, total, jnp.zeros((8, tile), F32)], 0)
        both = by_parts(dot_lanes, *split(both), owner)
        summed_ref[block, :hidden] += both[:hidden]
        totals[block] += both[hidden:]

    def step(index, carry):
        gather_up(jnp.maximum(index - 2, 0))
        score(jnp.maximum(index - 1, 0))
        choose(index)
        return carry

    lax.fori_loop(0, count + STAGES - 1, step, 0)
    summed_ref[...] = summed_ref[...] * 2.0
    for block in range(depth):
        summed_ref[block, hidden:] = selfs_ref[block] + totals[block, :8]
    over = jnp.where(totals[...] <= LARGEST, 0.0, 1.0)

    @pl.when(jnp.max(over) > 0.0)
    def _():
        def one(block, carry):
            summed_ref[block] = online_block(
                turned_ref, target_ref, table_ref, vector, depth, heads, block
            )
            return carry

        lax.fori_loop(0, depth, one, 0)


def online_block(turned_ref, target_ref, table_ref, vector, depth, heads, block):
    hidden, tile = vector.shape
    target = target_ref[block].astype(F32)
    target = target[:, :tile] + target[:, tile:]

    def of_pair(lane, carry):
        pair = lane * depth + block
        degree = jnp.max(turned_ref[pair].astype(F32), axis=0, keepdims=True)
        steps = (jnp.max(degree).astype(jnp.int32) + (RANKS - 1)) // RANKS

        def step(index, carry):
            top, total, summed = carry
            first = (index * RANKS).astype(F32)
            choice = jnp.concatenate(
                [
                    jnp.where(turned_ref[pair].astype(F32) == first + (r + 1), 1.0, 0.0).astype(BF16)
                    for r in range(RANKS)
                ],
                1,
            )
            both = dot(table_ref[pair], choice)
            values = both[:hidden] + both[hidden:]
            for r in range(RANKS):
                value = values[:, r * tile : (r + 1) * tile]
                half = value + target
                active = half * jnp.tanh(half) + half
                logits = jnp.where(first + r < degree, head_rows(active * vector, heads), NEGATIVE)
                new_top = jnp.maximum(top, logits)
                keep = jnp.exp(top - new_top)
                weight = jnp.exp(logits - new_top)
                total = total * keep + weight
                summed = summed * spread(keep, hidden) + spread(weight, hidden) * value
                top = new_top
            return top, total, summed

        return lax.fori_loop(0, steps, step, carry)

    zero = jnp.zeros((heads, tile), F32)
    top, total, summed = lax.fori_loop(
        0, turned_ref.shape[0] // depth, of_pair,
        (zero + NEGATIVE, zero, jnp.zeros((hidden, tile), F32)),
    )
    return jnp.concatenate([summed * 2.0, top, total], 0)


def backward_kernel(
    plan_in, turned_ref, bounds_ref, row_ref, target_ref, grads_ref, own_target_ref,
    own_source_ref, table_ref, vector_ref, logits_ref,
    grad_target_ref, grad_source_ref, grad_vector_ref,
    plan, plan_sem, chunk_block, chunk_first, collected, vector_sums, choice_in, target_in, grad_in, rows_in, owner_in,
    products_in, active_in, slope_in, *, slots, heads, columns, width,
):
    depth, hidden, tile = grad_target_ref.shape
    pairs = turned_ref.shape[0]
    load = pltpu.make_async_copy(plan_in, plan, plan_sem)
    load.start()
    half_vector = vector_ref[...] * 0.5
    for ref in (
        grad_target_ref, grad_source_ref, collected, vector_sums, choice_in, target_in, grad_in, rows_in,
        owner_in, products_in, active_in, slope_in,
    ):
        ref[...] = jnp.zeros_like(ref)
    me = lax.axis_index("src")
    grad_target_ref[me // width] = own_target_ref[...]
    grad_source_ref[me % width * columns + lax.axis_index("dst")] = own_source_ref[...]
    load.wait()
    count = list_chunks(plan, chunk_block, chunk_first, pairs, tile)

    def choose(index):
        block = chunk_block[index]
        here = lax.rem(block, depth)
        owner, near, left, choice, columns = virtual_rows(
            bounds_ref, row_ref, turned_ref, [target_ref[here], grads_ref[here]], block,
            chunk_first[index], tile,
        )
        for r in range(RANKS):
            choice_in[0, :, r * tile : (r + 1) * tile] = choice[r]
        target_in[...] = columns[0]
        grad_in[0] = columns[1]
        rows_in[0, :8] = near
        rows_in[0, 8:] = jnp.broadcast_to(left, (8, tile))
        owner_in[0] = owner

    def score(index):
        choice = choice_in[0]
        both = dot(table_ref[chunk_block[index]], choice)
        values = both[:hidden] + both[hidden:]
        target, grad = target_in[...], grad_in[0]
        for r in range(RANKS):
            value = values[:, r * tile : (r + 1) * tile]
            half = value + target
            risen = 1.0 + jnp.tanh(half)
            active = half * risen
            active_in[r] = active
            slope_in[r] = (risen + active * (2.0 - risen)) * half_vector
            products_in[r] = head_rows(value * grad, heads)
        grad_in[1] = grad
        choice_in[1] = choice
        rows_in[1] = rows_in[0]
        owner_in[1] = owner_in[0]

    def gather_up(index):
        block = chunk_block[index]
        log_total, delta, left = rows_in[1, :heads], rows_in[1, heads : 2 * heads], rows_in[1, 8:9]
        grad = grad_in[1]
        grad_target = jnp.zeros((hidden, tile), F32)
        grad_vector = vector_sums[...]
        outward = []
        for r in range(RANKS):
            weight = jnp.where(left > r, jnp.exp(logits_ref[index, r] - log_total), 0.0)
            grad_logit = spread(weight * (2.0 * products_in[r] - delta), hidden)
            grad_inner = grad_logit * slope_in[r]
            grad_target = grad_target + grad_inner
            grad_vector = grad_vector + grad_logit * active_in[r]
            outward.append(split(grad_inner + spread(weight, hidden) * grad))
        vector_sums[...] = grad_vector
        high, low = (jnp.concatenate(parts, 1) for parts in zip(*outward))
        collected[block] += by_parts(dot_lanes, high, low, choice_in[1])
        grad_target_ref[lax.rem(block, depth)] += by_parts(
            dot_lanes, *split(grad_target), owner_in[1]
        )

    def step(index, carry):
        gather_up(jnp.maximum(index - 2, 0))
        score(jnp.maximum(index - 1, 0))
        choose(index)
        return carry

    lax.fori_loop(0, count + STAGES - 1, step, 0)
    for pair in range(pairs):
        for slot in range(slots):
            place = pair // depth * columns + plan[pairs + pair * slots + slot]
            grad_source_ref[place] += collected[pair, :, slot * tile : (slot + 1) * tile]
    grad_vector_ref[...] = dot_lanes(jnp.ones((8, tile), F32), vector_sums[...], HIGH)


def on_device(
    sources, columns, features, source_weight, target_weight, attention_vector, attention_bias, residual_weight,
    norm_gain, norm_shift, neighbours, slot_valid, edge_mask, node_count, out_cotangent,
):
    tile, hidden = features.shape
    heads, head_size = attention_vector.shape
    slots = neighbours.shape[-1]
    wide = slots * tile
    depth, width = grid_of(sources)
    picks, valid, edge_mask = neighbours[0, 0].T, slot_valid[0, 0].T, edge_mask[0, 0]
    counts = node_count.T
    dma = pltpu.SemaphoreType.DMA
    smem = pl.BlockSpec(memory_space=SMEM)
    whole = pl.BlockSpec(memory_space=VMEM)
    hbm = pl.BlockSpec(memory_space=pltpu.HBM)
    limit = min(32 + sources * columns // 4, 60) * 1024 * 1024

    def shaped(*shape):
        return jax.ShapeDtypeStruct(shape, F32)

    def halves(*shape):
        return jax.ShapeDtypeStruct(shape, BF16)

    def communicating(number):
        return pltpu.CompilerParams(
            collective_id=number, has_side_effects=True, vmem_limit_bytes=limit
        )

    many = max(columns - 1, 1)
    more = max(width - 1, 1)
    edge_mask_tiles = (width, depth, slots, tile, tile)
    (
        by_line, by_side, target_all, source_all, turned, info, bounds, self_rows, selfs, source_own,
        target_own, vector, real, plan,
    ) = pl.pallas_call(
        functools.partial(gather_kernel, sources=sources, columns=columns, heads=heads),
        in_specs=[hbm] * 8,
        out_specs=[whole] * 13 + [smem],
        out_shape=[
            shaped(depth, tile, hidden), shaped(width * columns, tile, hidden),
            halves(depth, hidden, 2 * tile), halves(width * columns, hidden, 2 * tile),
            halves(sources, wide, tile), shaped(sources, 8, tile), shaped(sources, 2, tile, tile),
            halves(sources, 32, tile), shaped(depth, 8, tile), shaped(hidden, tile),
            shaped(hidden, tile), shaped(hidden, tile), shaped(8, tile),
            jax.ShapeDtypeStruct((sources * (1 + slots),), jnp.int32),
        ],
        scratch_shapes=[
            SMEM(picks.shape, jnp.int32), SMEM(valid.shape, jnp.int32), SMEM(counts.shape, jnp.int32),
            VMEM(attention_vector.shape, F32),
            VMEM(edge_mask_tiles, jnp.int32), VMEM((width, 2 * depth * slots, tile), F32),
            VMEM((more, 2 * depth * slots, tile), F32), VMEM((hidden, hidden), F32),
            VMEM((hidden, hidden), F32), VMEM((8, tile), F32), dma((8,)), dma((depth,)),
            *line_semaphores(depth), dma((many + more,)), dma((width * columns,)),
            dma((more, many)), dma((more, depth)), dma((width, depth)), dma((more,)), dma((width,)),
            *line_semaphores(depth),
        ],
        compiler_params=communicating(0),
    )(*[pltpu.with_memory_space_constraint(one, pltpu.HBM) for one in (
        picks, valid, counts, attention_vector, features, edge_mask, source_weight, target_weight
    )])

    most = sources * (-(-wide // RANKS)) + STAGES
    lists = [
        SMEM(plan.shape, jnp.int32), pltpu.SemaphoreType.DMA,
        SMEM((most,), jnp.int32), SMEM((most,), jnp.int32),
    ]
    params = pltpu.CompilerParams(vmem_limit_bytes=limit)
    slot_rows = VMEM((2, 16, tile), F32)
    owners = VMEM((2, tile, tile), BF16)
    by_rank = VMEM((RANKS, heads, tile), F32)
    summed, table, logits = pl.pallas_call(
        functools.partial(forward_kernel, heads=heads, columns=columns, slots=slots),
        in_specs=[whole] * 8,
        out_specs=[whole] * 3,
        out_shape=[
            shaped(depth, hidden + 8, tile), halves(sources, 2 * hidden, wide),
            shaped(most, RANKS, heads, tile),
        ],
        scratch_shapes=[
            *lists, VMEM((depth, 16, tile), F32), VMEM((wide, RANKS * tile), BF16),
            VMEM((hidden, tile), F32), slot_rows, owners, VMEM((hidden, RANKS * tile), F32),
        ],
        compiler_params=params,
    )(plan, turned, bounds, self_rows, target_all, selfs, source_all, vector)

    (
        output, log_rows, grads, own_target, own_source, rows, residual_grad, features_grad,
    ) = pl.pallas_call(
        functools.partial(middle_kernel, sources=sources, heads=heads),
        in_specs=[whole] * 12,
        out_specs=[whole] * 8,
        out_shape=[
            shaped(tile, hidden), halves(sources, 32, tile), halves(depth, hidden, 2 * tile),
            shaped(hidden, tile), shaped(hidden, tile), shaped(8, hidden),
            shaped(hidden, hidden), shaped(hidden, tile),
        ],
        scratch_shapes=[
            VMEM((depth, hidden, tile), F32), VMEM((depth, 8, tile), F32), VMEM((8, tile), F32),
            *line_semaphores(depth), *line_semaphores(depth),
            *reduce_scratch(depth, hidden + 8, tile),
        ],
        compiler_params=communicating(1),
    )(
        real, summed, features, source_own, target_own, info, residual_weight,
        vector, attention_bias.reshape(1, hidden), norm_gain.reshape(1, hidden),
        norm_shift.reshape(1, hidden), out_cotangent,
    )

    grad_targets, grad_sources, vector_grad = pl.pallas_call(
        functools.partial(backward_kernel, slots=slots, heads=heads, columns=columns, width=width),
        in_specs=[whole] * 11,
        out_specs=[whole] * 3,
        out_shape=[
            shaped(depth, hidden, tile), shaped(width * columns, hidden, tile), shaped(8, hidden)
        ],
        scratch_shapes=[
            *lists, VMEM((sources, hidden, wide), F32), VMEM((hidden, tile), F32),
            VMEM((2, wide, RANKS * tile), BF16), VMEM((hidden, tile), F32),
            VMEM((2, hidden, tile), F32), slot_rows, owners, by_rank,
            VMEM((RANKS, hidden, tile), F32), VMEM((RANKS, hidden, tile), F32),
        ],
        compiler_params=params,
    )(
        plan, turned, bounds, log_rows, target_all, grads, own_target, own_source, table,
        vector, logits,
    )

    step = 8 * sources * columns
    stacked = -(-hidden // step) * step
    across = columns // 2
    heights = [2 * stacked, stacked]
    group = [columns - 1, sources - 1]
    back = [1, max(across - 1, 1), sources - 1]

    grad_features, pair, single, sums = pl.pallas_call(
        functools.partial(last_kernel, sources=sources, columns=columns),
        in_specs=[whole] * 10,
        out_specs=[whole] * 4,
        out_shape=[
            shaped(hidden, tile), *[shaped(height, hidden) for height in heights], shaped(8, hidden)
        ],
        scratch_shapes=[
            [VMEM((height, hidden), F32) for height in heights],
            [
                [
                    VMEM((columns - 1, height // columns, hidden), F32),
                    VMEM((sources - 1, height // columns // sources, hidden), F32),
                ]
                for height in heights
            ],
            [VMEM((n, 8, hidden), F32) for n in group],
            *[[dma((2, n)) for n in group] for _ in range(2)],
            *[[dma((n,)) for n in group] for _ in range(2)],
            *[[dma((2, n)) for n in back] for _ in range(2)],
            VMEM((width * across, hidden, tile), F32), VMEM((width * across, hidden, tile), F32),
            dma((width * across,)), dma((width * across,)),
            VMEM((more * across, hidden, tile), F32), VMEM((across, hidden, tile), F32),
            dma((more * across,)), dma((more * across,)),
            VMEM((max(across - 1, 1), hidden, tile), F32), dma((max(across - 1, 1),)),
            dma((max(across - 1, 1),)),
            *reduce_scratch(depth, hidden, tile),
        ],
        compiler_params=communicating(2),
    )(
        grad_targets, grad_sources, vector_grad, rows, by_line, by_side, residual_grad,
        features_grad, source_weight, target_weight,
    )

    line = shaped(1, hidden)
    square = shaped(hidden, hidden)
    output, *rest = pl.pallas_call(
        outputs_kernel,
        in_specs=[whole] * 5,
        out_specs=[whole] * 9,
        out_shape=[
            shaped(tile, hidden), shaped(tile, hidden), square, square, shaped(heads, head_size),
            line, square, line, line,
        ],
        compiler_params=pltpu.CompilerParams(vmem_limit_bytes=limit),
    )(output, grad_features, pair, single, sums)
    return (output, *[one.reshape(hidden) if one.shape[0] == 1 else one for one in rest])


def solution(mesh):
    rows = P(("src", "dst"), None)
    placed = (
        rows, P(), P(), P(), P(), P(), P(), P(),
        P("src", "dst", None, None), P("src", "dst", None, None),
        P("src", "dst", None, None, None, None), P(), rows,
    )
    return jax.shard_map(
        functools.partial(on_device, mesh.shape["src"], mesh.shape["dst"]),
        mesh=mesh, in_specs=placed,
        out_specs=(rows, rows, P(), P(), P(), P(), P(), P(), P()), check_vma=False,
    )
```
